256 devices in a mesh: group: 8 (over x, core), tensor: 8 (over z), rep: 4 (over y).
Axes of the slice: x: 4, y: 4, z: 8, core: 2. Of those that a mesh axis runs over, the one named last changes fastest.
Arguments:
- probe_vectors: bfloat16 [512, 64, 128], P(('group', 'rep'), 'tensor'), may hold values from -500 to 500
- stored_lookup_vectors: bfloat16 [512, 8, 512, 128], P(('group', 'rep'), 'tensor'), may hold values from -6 to 6
- stored_content_vectors: bfloat16 [512, 8, 512, 128], P(('group', 'rep'), 'tensor'), may hold values from -6 to 6
- fresh_lookup_vector: bfloat16 [512, 8, 128], P(('group', 'rep'), 'tensor'), may hold values from -6 to 6
- fresh_content_vector: bfloat16 [512, 8, 128], P(('group', 'rep'), 'tensor'), may hold values from -6 to 6
- history_counts: int32 [512], P(('group', 'rep')), may hold values from 1 to 512, as said below
- mixing_matrix: bfloat16 [8192, 8192], P('tensor', ('group', 'rep')), may hold values from -0.25 to 0.25
- skip_stream: bfloat16 [512, 8192], P(('group', 'rep'), 'tensor'), may hold values from -8 to 8
- closing_multiplier: bfloat16 [8192], P('tensor'), may hold values from 0.25 to 1.75
- lexicon_matrix: bfloat16 [8192, 131072], P(None, ('group', 'tensor', 'rep')), may hold values from -0.088388348 to 0.088388348
- sharpening_factor: float32 [512], replicated, may hold values from 0.5 to 20
- desired_perplexity: float32 [512], replicated, may hold values from 6 to 12
- chosen_symbols: int32 [512], replicated, may hold values from 0 to 131071
Outputs:
- hidden: bfloat16 [512, 8192], P(('group', 'rep'), 'tensor')
- next_targets: float32 [512], replicated
- surprise: float32 [512], replicated
The draws below stay inside these ranges and needn't reach their ends.
Inputs may be any that keep to these rules, and one draw needn't show every extreme that they name: `history_counts`: each row holds at least one cached position; some row holds 512.
All inputs are finite; a program needn't handle non-finite values.
Results may differ from the reference program's by a relative error of at most 0.0063.
Values may be sent and summed in bfloat16 or wider, within the bound.
No kernel may reach another device: no remote copies, remote signals or barrier semaphores. Data moves between devices by JAX's collectives and lax.ppermute only.
A program may use at most 128 MiB of HBM per device.

```python
import math
import jax
import jax.numpy as jnp
from jax import lax

D = 8192
HEADS = 64
KV_HEADS = 8
HEAD_DIM = 128
CACHE = 512
ROWS = 512
VOCAB = 131072


def shared_rows(key):
    id_key = jax.random.fold_in(key, 11)
    dir_key = jax.random.fold_in(key, 13)
    picked = jax.random.randint(id_key, (ROWS,), 0, VOCAB)
    picked = picked.at[0].set(0).at[ROWS - 1].set(VOCAB - 1)
    direction = jnp.clip(jax.random.normal(dir_key, (ROWS, D), jnp.float32), -3.0, 3.0)
    return (picked, direction)


def draw_probe_vectors(key, part):
    key = jax.random.fold_in(key, 1)
    base = jax.random.normal(key, (ROWS, HEADS, HEAD_DIM), jnp.float32)
    return jnp.clip(base, -500.0, 500.0).astype(jnp.bfloat16)


def draw_history_counts(key, part):
    key = jax.random.fold_in(key, 3)
    picks = jax.random.randint(key, (ROWS,), 1, CACHE + 1)
    history_counts = 1 + (picks * picks - 1) // CACHE
    return history_counts.at[0].set(CACHE).astype(jnp.int32)


def draw_sharpening_factor(key, part):
    key = jax.random.fold_in(key, 5)
    upper = jnp.log(8.0)
    spread = jax.random.uniform(key, (ROWS,), jnp.float32, jnp.log(0.5), upper)
    return jnp.exp(spread).astype(jnp.float32)


def draw_skip_stream(key, part):
    picked, direction = shared_rows(key)
    key = jax.random.fold_in(key, 9)
    fraction = jnp.arange(D, dtype=jnp.float32)[None, :] / D
    row_gain = jax.random.uniform(jax.random.fold_in(key, 2), (ROWS, 1), jnp.float32, 0.7, 1.4)
    base = jax.random.normal(key, (ROWS, D), jnp.float32)
    scale = 0.2 * jnp.exp(fraction * jnp.log(15.0))
    return jnp.clip(base * scale * row_gain + 0.6 * direction, -8.0, 8.0).astype(jnp.bfloat16)


def draw_lexicon_matrix(key, part):
    picked, direction = shared_rows(key)
    key = jax.random.fold_in(key, 17)
    limit = 8.0 * D ** (-0.5)
    base = jax.random.normal(key, (D, VOCAB), jnp.float32) * (2.0 * D ** (-0.5))
    strength = jax.random.uniform(jax.random.fold_in(key, 2), (ROWS,), jnp.float32, 0.22, 0.6)
    columns = direction.T * strength[None, :] * D ** (-0.5)
    lexicon = base.at[:, picked].add(columns)
    return jnp.clip(lexicon, -limit, limit).astype(jnp.bfloat16)


def draw_chosen_symbols(key, part):
    picked, direction = shared_rows(key)
    return picked.astype(jnp.int32)


def level_of(key, shape, split, low, high):
    factor_of = 1.0
    for dim, blocks in split:
        steps = jax.random.uniform(jax.random.fold_in(jax.random.fold_in(key, 6), dim), (blocks,), jnp.float32, low / len(split), high / len(split))
        factor_of = factor_of * jnp.repeat(jnp.exp(steps), shape[dim] // blocks).reshape((-1,) + (1,) * (len(shape) - 1 - dim))
    return factor_of


def bell_draw(key, extent, scale, most, cuts=(), held_as=jnp.bfloat16):
    factor_of = level_of(key, extent, cuts, -0.22, 0.18) if cuts else 1.0
    drawn = jax.random.normal(key, extent, jnp.float32) * scale * factor_of
    return jnp.minimum(jnp.maximum(drawn, -most), most).astype(held_as)


def setup_inputs(seed: int = 0) -> dict:
    seeds = jax.random.split(jax.random.key(seed), 14)
    return {
        "probe_vectors": draw_probe_vectors(jax.random.fold_in(seeds[13], 71), 0),
        "stored_lookup_vectors": bell_draw(seeds[1], (ROWS, KV_HEADS, CACHE, HEAD_DIM), 1.0, 6.0, ((0, 32), (1, 8))),
        "stored_content_vectors": bell_draw(seeds[2], (ROWS, KV_HEADS, CACHE, HEAD_DIM), 1.0, 6.0, ((0, 32), (1, 8))),
        "fresh_lookup_vector": bell_draw(seeds[3], (ROWS, KV_HEADS, HEAD_DIM), 1.0, 6.0, ((0, 32), (1, 8))),
        "fresh_content_vector": bell_draw(seeds[4], (ROWS, KV_HEADS, HEAD_DIM), 1.0, 6.0, ((0, 32), (1, 8))),
        "history_counts": draw_history_counts(jax.random.fold_in(seeds[13], 71), 0),
        "mixing_matrix": bell_draw(seeds[6], (HEADS * HEAD_DIM, D), (HEADS * HEAD_DIM // 16) ** -0.5, 0.25, ((0, 8), (1, 32))),
        "skip_stream": draw_skip_stream(jax.random.fold_in(seeds[13], 71), 0),
        "closing_multiplier": jnp.clip(1.0 + 0.15 * jax.random.normal(seeds[8], (D,), jnp.float32), 0.25, 1.75).astype(jnp.bfloat16),
        "lexicon_matrix": draw_lexicon_matrix(jax.random.fold_in(seeds[13], 71), 0),
        "sharpening_factor": draw_sharpening_factor(jax.random.fold_in(seeds[13], 71), 0),
        "desired_perplexity": jnp.clip(jax.random.uniform(seeds[11], (ROWS,), jnp.float32, 6.0, 12.0), 6.0, 12.0),
        "chosen_symbols": draw_chosen_symbols(jax.random.fold_in(seeds[13], 71), 0),
    }


cut_slope = 4.0

def attend_row(item):
    probe_vectors, keys, values, own_key, own_value, length = item
    group = HEADS // KV_HEADS
    grouped_query_rows = probe_vectors.astype(jnp.float32).reshape(KV_HEADS, group, HEAD_DIM)
    score_scale = 1.0 / math.sqrt(HEAD_DIM)
    scores = jnp.einsum('kgd,kld->kgl', grouped_query_rows, keys.astype(jnp.float32)) * score_scale
    self_entry = jnp.einsum('kgd,kd->kg', grouped_query_rows, own_key.astype(jnp.float32)) * score_scale
    position = jnp.arange(CACHE, dtype=jnp.int32)[None, None, :]
    live = position < length
    top = jnp.maximum(lax.optimization_barrier(jnp.max(jnp.where(live, scores, -1e+30), axis=2)), self_entry)
    expo = jnp.where(live, jnp.exp(scores - top[..., None]), 0.0)
    own_expo = jnp.exp(self_entry - top)
    total = lax.optimization_barrier(jnp.sum(expo, axis=2)) + own_expo
    attention_weights = lax.optimization_barrier(expo.astype(jnp.bfloat16)).astype(jnp.float32)
    self_weight = lax.optimization_barrier(own_expo.astype(jnp.bfloat16)).astype(jnp.float32)
    accum = jnp.einsum('kgl,kld->kgd', attention_weights, values.astype(jnp.float32))
    accum = accum + jnp.einsum('kg,kd->kgd', self_weight, own_value.astype(jnp.float32))
    return (accum / total[..., None]).reshape(HEADS * HEAD_DIM).astype(jnp.bfloat16)

def reference(probe_vectors, stored_lookup_vectors, stored_content_vectors, fresh_lookup_vector, fresh_content_vector, history_counts, mixing_matrix, skip_stream, closing_multiplier, lexicon_matrix, sharpening_factor, desired_perplexity, chosen_symbols):
    attn = lax.map(attend_row, (probe_vectors, stored_lookup_vectors, stored_content_vectors, fresh_lookup_vector, fresh_content_vector, history_counts))
    projected = jnp.dot(attn, mixing_matrix, preferred_element_type=jnp.float32)
    hidden = (skip_stream.astype(jnp.float32) + projected).astype(jnp.bfloat16)
    wide = hidden.astype(jnp.float32)
    mean_sq = lax.optimization_barrier(jnp.mean(wide * wide, axis=1))
    rescaled_stream = (wide * lax.rsqrt(mean_sq + 1e-05)[:, None] * closing_multiplier.astype(jnp.float32)).astype(jnp.bfloat16)
    unnormalized_odds = jnp.dot(rescaled_stream, lexicon_matrix, preferred_element_type=jnp.float32) * sharpening_factor[:, None]
    top = lax.optimization_barrier(jnp.max(unnormalized_odds, axis=1))
    lognorm = top + jnp.log(lax.optimization_barrier(jnp.sum(jnp.exp(unnormalized_odds - top[:, None]), axis=1)))
    logp = unnormalized_odds - lognorm[:, None]
    bits = -logp / math.log(2.0)
    logw = logp + jax.nn.log_sigmoid(cut_slope * (desired_perplexity[:, None] - bits))
    kept = lax.optimization_barrier(jnp.sum(jnp.exp(logw), axis=1))
    hit = jnp.arange(VOCAB, dtype=jnp.int32)[None, :] == chosen_symbols[:, None]
    token_logit = lax.optimization_barrier(jnp.sum(jnp.where(hit, unnormalized_odds, 0.0), axis=1))
    token_logp = token_logit - lognorm
    token_logw = token_logp + jax.nn.log_sigmoid(cut_slope * (desired_perplexity + token_logp / math.log(2.0)))
    surprise = -(token_logw - jnp.log(kept)) / math.log(2.0)
    next_targets = desired_perplexity - 0.1 * (surprise - 5.0)
    return (hidden, next_targets, surprise)
```

```python
import functools
import math

import jax
import jax.numpy as jnp
from jax import lax
from jax.experimental import pallas as pl
from jax.experimental.pallas import tpu as pltpu
from jax.sharding import Mesh
from jax.sharding import PartitionSpec as P

cut_slope = 4.0
LN2 = math.log(2.0)
F32 = jnp.float32
BF16 = jnp.bfloat16
PLANE = ("x", "core", "rep")
SAME_CORE = ("x", "tensor", "rep")


def attend(
    probe_vectors,
    stored_lookup_vectors,
    stored_content_vectors,
    fresh_lookup_vector,
    fresh_content_vector,
    history_counts,
):
    rows, kv_local, cache_len, head_dim = stored_lookup_vectors.shape
    heads_local = probe_vectors.shape[1]
    grouped_query_rows = probe_vectors.reshape(rows, kv_local, heads_local // kv_local, head_dim)
    score_scale = 1.0 / math.sqrt(head_dim)
    self_entry = (
        jnp.einsum(
            "mjqo,mjo->mjq",
            grouped_query_rows,
            fresh_lookup_vector,
            preferred_element_type=jnp.float32,
        )
        * score_scale
    )
    scores = (
        jnp.einsum(
            "bkgd,bkld->bkgl",
            grouped_query_rows,
            stored_lookup_vectors,
            preferred_element_type=jnp.float32,
        )
        * score_scale
    )
    position = lax.broadcasted_iota(jnp.int32, (1, 1, 1, cache_len), 3)
    live = position < history_counts[:, None, None, None]
    top = jnp.maximum(jnp.max(jnp.where(live, scores, -1e30), axis=3), self_entry)
    expo = jnp.where(live, jnp.exp(scores - top[..., None]), 0.0)
    total = jnp.sum(expo, axis=3)
    accum = jnp.einsum(
        "bkgl,bkld->bkgd",
        expo.astype(jnp.bfloat16),
        stored_content_vectors,
        preferred_element_type=jnp.float32,
    )
    own_expo = jnp.exp(self_entry - top)
    total = total + own_expo
    accum = accum + jnp.einsum(
        "vct,vcn->vctn",
        own_expo.astype(jnp.bfloat16),
        fresh_content_vector,
        preferred_element_type=jnp.float32,
    )
    return (accum / total[..., None]).reshape(rows, heads_local * head_dim).astype(jnp.bfloat16)


def turn(shift):
    pairs = []
    for x in range(4):
        for c in range(2):
            for y in range(4):
                here = (x * 2 + c) * 4 + y
                if c == 0:
                    there = (((x + shift) % 4) * 2 + c) * 4 + y
                else:
                    there = (x * 2 + c) * 4 + (y + shift) % 4
                pairs.append((here, there))
    return pairs


def turn_other(shift):
    pairs = []
    for x in range(4):
        for c in range(2):
            for y in range(4):
                here = (x * 2 + c) * 4 + y
                if c == 1:
                    there = (((x + shift) % 4) * 2 + c) * 4 + y
                else:
                    there = (x * 2 + c) * 4 + (y + shift) % 4
                pairs.append((here, there))
    return pairs


def swap_core(value):
    return lax.ppermute(value, "core", [(0, 1), (1, 0)])


def head_body(
    steps,
    first,
    last,
    table,
    h_ref,
    lo_a,
    lo_b,
    lp_a,
    lp_b,
    m_a,
    m_b,
    *rest,
):
    rest = list(rest)
    if not first:
        z_in, sq_in = rest[:2]
        rest = rest[2:]
    if last:
        sharp, chosen, z_out, lse_out, tok_out, sq_acc = rest
        sq_ref = sq_acc
    else:
        z_out, sq_ref = rest
    step = pl.program_id(0)

    @pl.when(step == 0)
    def _():
        if first:
            z_out[...] = jnp.zeros_like(z_out)
            sq_ref[...] = jnp.zeros_like(sq_ref)
        else:
            z_out[...] = z_in[...]
            sq_ref[...] = sq_in[...]

    wide = h_ref[0].astype(F32)
    half = wide.shape[1] // 2
    squares = wide * wide
    sq_ref[...] += (
        squares[:, 0:128] + squares[:, 128:256] + squares[:, 256:384] + squares[:, 384:512]
    )
    xa = (wide[:, :half] * m_a[0].astype(F32)).astype(BF16)
    xb = (wide[:, half:] * m_b[0].astype(F32)).astype(BF16)
    cols = lo_a.shape[1]
    z_out[:, :cols] += jnp.dot(xa, lo_a[...], preferred_element_type=F32) + jnp.dot(
        xb, lo_b[...], preferred_element_type=F32
    )
    z_out[:, cols:] += jnp.dot(xa, lp_a[...], preferred_element_type=F32) + jnp.dot(
        xb, lp_b[...], preferred_element_type=F32
    )

    if last:

        @pl.when(step == steps - 1)
        def _():
            total = jnp.sum(sq_ref[...], axis=1, keepdims=True)
            scale = lax.rsqrt(total / 8192.0 + 1e-05) * sharp[...]
            z = z_out[...] * scale
            z_out[...] = z
            top = jnp.max(z, axis=1, keepdims=True)
            mass = jnp.sum(jnp.exp(z - top), axis=1, keepdims=True)
            lse_out[...] = jnp.transpose(jnp.broadcast_to(top + jnp.log(mass), (z.shape[0], 128)))
            spot = lax.broadcasted_iota(jnp.int32, z.shape, 1)
            token = jnp.sum(jnp.where(spot == chosen[...], z, 0.0), axis=1, keepdims=True)
            tok_out[...] = jnp.transpose(jnp.broadcast_to(token, (z.shape[0], 128)))


def head_call(blocks, table, lex_own, lex_peer, gain, state, closing):
    steps, rows, width = blocks.shape
    half = width // 2
    cols = lex_own.shape[1]
    first, last = state is None, closing is not None
    whole = lambda *shape: pl.BlockSpec(shape, lambda i, t: (0,) * len(shape))
    in_specs = [
        pl.BlockSpec((1, rows, width), lambda i, t: (i, 0, 0)),
        pl.BlockSpec((half, cols), lambda i, t: (t[2 * i], 0)),
        pl.BlockSpec((half, cols), lambda i, t: (t[2 * i + 1], 0)),
        pl.BlockSpec((half, cols), lambda i, t: (t[2 * i], 0)),
        pl.BlockSpec((half, cols), lambda i, t: (t[2 * i + 1], 0)),
        pl.BlockSpec((1, 1, half), lambda i, t: (t[2 * i], 0, 0)),
        pl.BlockSpec((1, 1, half), lambda i, t: (t[2 * i + 1], 0, 0)),
    ]
    operands = [blocks, lex_own, lex_own, lex_peer, lex_peer, gain, gain]
    scratch = []
    if not first:
        in_specs += [whole(rows, 2 * cols), whole(rows, 128)]
        operands += list(state)
    out_shape = [jax.ShapeDtypeStruct((rows, 2 * cols), F32)]
    out_specs = [whole(rows, 2 * cols)]
    if last:
        in_specs += [whole(rows, 1), whole(rows, 1)]
        operands += list(closing)
        out_shape += [jax.ShapeDtypeStruct((128, rows), F32)] * 2
        out_specs += [whole(128, rows)] * 2
        scratch = [pltpu.VMEM((rows, 128), F32)]
    else:
        out_shape += [jax.ShapeDtypeStruct((rows, 128), F32)]
        out_specs += [whole(rows, 128)]
    return pl.pallas_call(
        functools.partial(head_body, steps, first, last),
        grid_spec=pltpu.PrefetchScalarGridSpec(
            num_scalar_prefetch=1,
            grid=(steps,),
            in_specs=in_specs,
            out_specs=out_specs,
            scratch_shapes=scratch,
        ),
        out_shape=out_shape,
        compiler_params=pltpu.CompilerParams(vmem_limit_bytes=24 * 1024 * 1024),
        cost_estimate=pl.CostEstimate(
            flops=4 * rows * steps * width * cols,
            bytes_accessed=steps * (rows * width * 2 + width * cols * 4) + rows * cols * 8,
            transcendentals=0,
        ),
    )(table, *operands)


def mass_body(z_ref, lse_ref, level_ref, kept_out, norm_out):
    parts = lse_ref[...]
    top = jnp.max(parts, axis=0, keepdims=True)
    norm = top + jnp.log(jnp.sum(jnp.exp(parts - top), axis=0, keepdims=True))
    norm_out[...] = norm
    column = jnp.transpose(jnp.broadcast_to(norm, parts.shape))[:, :1]
    logp = z_ref[...] - column
    gate = cut_slope * (level_ref[...] + logp * (1.0 / LN2))
    kept = jnp.sum(jnp.exp(logp) / (1.0 + jnp.exp(-gate)), axis=1, keepdims=True)
    kept_out[...] = jnp.transpose(jnp.broadcast_to(kept, (kept.shape[0], 128)))


def mass_call(z, lse, level):
    rows = z.shape[0]
    return pl.pallas_call(
        mass_body,
        out_shape=[
            jax.ShapeDtypeStruct((128, rows), F32),
            jax.ShapeDtypeStruct((1, rows), F32),
        ],
        compiler_params=pltpu.CompilerParams(vmem_limit_bytes=24 * 1024 * 1024),
    )(z, lse, level)


def shards(
    probe_vectors,
    stored_lookup_vectors,
    stored_content_vectors,
    fresh_lookup_vector,
    fresh_content_vector,
    history_counts,
    mixing_matrix,
    skip_stream,
    closing_multiplier,
    lexicon_matrix,
    sharpening_factor,
    desired_perplexity,
    chosen_symbols,
):
    x, c, t, y = (lax.axis_index(name) for name in ("x", "core", "tensor", "rep"))
    mix_peer = swap_core(mixing_matrix)
    lex_peer = swap_core(lexicon_matrix)

    attn = attend(
        probe_vectors,
        stored_lookup_vectors,
        stored_content_vectors,
        fresh_lookup_vector,
        fresh_content_vector,
        history_counts,
    )

    skip_blocks = skip_stream.reshape(16, 4, 256).transpose(1, 0, 2)
    skip_sent = jnp.broadcast_to(skip_blocks[None], (4, 4, 16, 256)).reshape(16, 16, 256)
    sent = jnp.concatenate([jnp.broadcast_to(attn[None], (16, 16, 1024)), skip_sent], axis=2)
    got = lax.all_to_all(sent, ("x", "rep"), 0, 0, tiled=True).reshape(256, 1280)
    every_attn = got[:, :1024]
    skip_got = got[:, 1024:]

    part_own = jnp.dot(every_attn, mixing_matrix, preferred_element_type=F32).astype(BF16)
    part_peer = jnp.dot(every_attn, mix_peer, preferred_element_type=F32).astype(BF16)
    gain_row = jnp.broadcast_to(closing_multiplier.reshape(1, 8, 128), (8, 8, 128))
    gain_sent = jnp.concatenate([gain_row, jnp.zeros((8, 24, 128), BF16)], axis=1)
    sent = jnp.concatenate(
        [
            part_own.reshape(8, 32, 256),
            part_peer.reshape(8, 32, 256),
            skip_got.reshape(8, 32, 256),
            gain_sent,
        ],
        axis=2,
    )
    got = lax.all_to_all(sent, "tensor", 0, 0, tiled=True)
    gain = got[:, :8, 768:].reshape(32, 1, 256)
    sums = jnp.sum(got[:, :, :512].astype(F32), axis=0)
    skip_own = lax.dynamic_index_in_dim(got[:, :, 512:768], 2 * x + c, 0, keepdims=False)
    skip_peer = lax.dynamic_index_in_dim(got[:, :, 512:768], 2 * x + 1 - c, 0, keepdims=False)
    skip = jnp.concatenate([skip_own, skip_peer], axis=1).astype(F32)
    piece = (skip + sums).astype(BF16)

    sent = jnp.broadcast_to(piece[None], (8, 32, 512))
    block = lax.all_to_all(sent, "tensor", 0, 0, tiled=True).reshape(256, 512)
    near = [block] + [lax.ppermute(block, PLANE, turn_other(s)) for s in (1, -1, 2)]
    stack = jnp.stack(near)
    from_left = lax.ppermute(stack, PLANE, turn(1))
    from_right = lax.ppermute(stack, PLANE, turn(-1))
    far_a = lax.ppermute(from_left[:2], PLANE, turn(1))
    far_b = lax.ppermute(from_right[2:], PLANE, turn(-1))

    order = []
    for far in (0, -1, 1, 2):
        for side in (0, -1, 1, 2):
            bx = jnp.where(c == 0, x + far, x + side) % 4
            by = jnp.where(c == 0, y + side, y + far) % 4
            order += [(bx * 2 + c) * 4 + by, (bx * 2 + 1 - c) * 4 + by]
    table = jnp.stack(order).astype(jnp.int32)

    mine = lambda v: lax.dynamic_index_in_dim(v.reshape(4, 2, 64), c, 1, keepdims=False).reshape(256)
    sharp = mine(sharpening_factor)
    level = mine(desired_perplexity)
    picks = mine(chosen_symbols)
    base_own = (((x * 2 + c) * 8 + t) * 4 + y) * 512
    base_peer = (((x * 2 + 1 - c) * 8 + t) * 4 + y) * 512
    in_own = (picks >= base_own) & (picks < base_own + 512)
    in_peer = (picks >= base_peer) & (picks < base_peer + 512)
    spot = jnp.where(in_own, picks - base_own, jnp.where(in_peer, picks - base_peer + 512, -1))

    near_blocks = jnp.concatenate([stack, from_left, from_right])
    far_blocks = jnp.concatenate([far_a, far_b])
    state = head_call(near_blocks, table[:24], lexicon_matrix, lex_peer, gain, None, None)
    z, lse, tok = head_call(
        far_blocks,
        table[24:],
        lexicon_matrix,
        lex_peer,
        gain,
        state,
        (sharp[:, None], spot[:, None]),
    )
    every_lse = lax.all_to_all(
        lse.reshape(128, 2, 128), SAME_CORE, 0, 0, tiled=True
    ).reshape(128, 256)
    kept, norm = mass_call(z, every_lse, level[:, None])
    sent = jnp.concatenate([kept, tok], axis=1).reshape(128, 4, 128)
    got = lax.all_to_all(sent, SAME_CORE, 0, 0, tiled=True)
    kept, tok = jnp.sum(got, axis=0).reshape(2, 256)
    token_logp = tok - norm.reshape(256)
    token_logw = token_logp + jax.nn.log_sigmoid(cut_slope * (level + token_logp / LN2))
    mine_out = -(token_logw - jnp.log(kept)) / LN2
    peer_out = swap_core(mine_out)
    even = jnp.where(c == 0, mine_out, peer_out).reshape(4, 64)
    odd = jnp.where(c == 0, peer_out, mine_out).reshape(4, 64)
    surprise = jnp.stack([even, odd], axis=1).reshape(512)
    next_targets = desired_perplexity - 0.1 * (surprise - 5.0)

    every_block = jnp.concatenate([near_blocks, far_blocks])
    rows = lax.dynamic_slice_in_dim(every_block, (x * 4 + y) * 16, 16, 1)
    half = lax.dynamic_slice_in_dim(rows, jnp.where(t % 2 == c, 0, 256), 256, 2)
    place = lambda delta: jnp.array([0, 2, 3, 1], jnp.int32)[delta % 4]
    pieces = []
    for yb in range(4):
        dx, dy = t // 2 - x, yb - y
        far = jnp.where(c == 0, dx, dy)
        side = jnp.where(c == 0, dy, dx)
        pieces.append(
            lax.dynamic_index_in_dim(half, place(far) * 4 + place(side), 0, keepdims=False)
        )
    hidden = jnp.concatenate(pieces, axis=1)
    return (hidden, next_targets, surprise)


def solution(mesh):
    fine = Mesh(mesh.devices.reshape(4, 2, 8, 4), ("x", "core", "tensor", "rep"))
    rows = ("x", "core", "rep")
    placed = (
        P(rows, "tensor", None),
        P(rows, "tensor", None, None),
        P(rows, "tensor", None, None),
        P(rows, "tensor", None),
        P(rows, "tensor", None),
        P(rows),
        P("tensor", rows),
        P(rows, "tensor"),
        P("tensor"),
        P(None, ("x", "core", "tensor", "rep")),
        P(),
        P(),
        P(),
    )
    return jax.shard_map(
        shards,
        mesh=fine,
        in_specs=placed,
        out_specs=(P(rows, "tensor"), P(), P()),
        check_vma=False,
    )
```

```python
import functools
import math

import jax
import jax.numpy as jnp
from jax import lax
from jax.experimental import pallas as pl
from jax.experimental.pallas import tpu as pltpu
from jax.sharding import Mesh
from jax.sharding import PartitionSpec as P

cut_slope = 4.0
LN2 = math.log(2.0)
F32 = jnp.float32
BF16 = jnp.bfloat16
PLANE = ("x", "core", "rep")
EVERY = ("x", "core", "tensor", "rep")
SAME_CORE = ("x", "tensor", "rep")
LIMIT = 16 * 1024 * 1024


def place():
    return tuple(lax.axis_index(name) for name in ("x", "core", "tensor", "rep"))


def number(far, side, half):
    x, c, _, y = place()
    even = c == 0
    bx = jnp.where(even, x + (far % 4), x + (side % 4)) % 4
    by = jnp.where(even, y + (side % 4), y + (far % 4)) % 4
    return (bx * 2 + (c if half == 0 else 1 - c)) * 4 + by


def column_of(table, held):
    c = lax.axis_index("core")
    held[...] = jnp.transpose(jnp.concatenate([table, jnp.zeros((124, 128), F32)]))
    start = pl.multiple_of(c * 64, 64)
    return jnp.concatenate([held[pl.ds(start, 64), i : i + 1] for i in range(4)])


LOWS, HIGHS = (0, -1), (1, 2)
BLOCKS = [
    (far, side)
    for far, sides in (
        (0, LOWS),
        (0, HIGHS),
        (-1, LOWS),
        (1, HIGHS),
        (-1, HIGHS),
        (1, LOWS),
        (2, LOWS),
        (2, HIGHS),
    )
    for side in sides
]


def in_hbm(value):
    return pltpu.with_memory_space_constraint(value, pltpu.HBM)


def in_vmem(value):
    return pltpu.with_memory_space_constraint(value, pltpu.VMEM)


def attend_body(
    counts, q_ref, k_hbm, v_hbm, own_k_ref, own_v_ref, skip_ref, mix, out_ref, mix_out, *scratch
):
    k_ref, v_ref, own_k, own_v, held, sems, mix_sem = scratch
    rows = 4
    groups = k_ref.shape[0] // rows
    score_scale = 1.0 / math.sqrt(k_ref.shape[3])
    copies = []
    for group in range(groups):
        span = pl.ds(group * rows, rows)
        pair = [
            pltpu.make_async_copy(k_hbm.at[span], k_ref.at[span], sems.at[2 * group]),
            pltpu.make_async_copy(v_hbm.at[span], v_ref.at[span], sems.at[2 * group + 1]),
        ]
        for copy in pair:
            copy.start()
        copies.append(pair)
    mix_copy = pltpu.make_async_copy(mix, mix_out, mix_sem)
    mix_copy.start()
    own_k[...] = own_k_ref[...].astype(F32)
    own_v[...] = own_v_ref[...].astype(F32)
    for there in range(16):
        block = there % 4
        out_ref[there, :, 1024:] = skip_ref[:, block * 256 : (block + 1) * 256]

    for group in range(groups):
        first = group * rows
        spread = lambda ref: jnp.concatenate(
            [jnp.broadcast_to(ref[first + row : first + row + 1], (8, 128)) for row in range(rows)]
        )
        q = q_ref[first : first + rows].reshape(rows * 8, 128)
        own = score_scale * jnp.sum(q.astype(F32) * spread(own_k), axis=1, keepdims=True)
        copies[group][0].wait()
        scores = score_scale * jnp.concatenate(
            [
                lax.dot_general(
                    q_ref[first + row],
                    k_ref[first + row, 0],
                    (((1,), (1,)), ((), ())),
                    preferred_element_type=F32,
                )
                for row in range(rows)
            ]
        )
        position = lax.broadcasted_iota(jnp.int32, (8, scores.shape[1]), 1)
        live = jnp.concatenate([position < counts[first + row] for row in range(rows)])
        top = jnp.maximum(jnp.max(jnp.where(live, scores, -1e30), axis=1, keepdims=True), own)
        expo = jnp.where(live, jnp.exp(scores - top), 0.0)
        own_expo = jnp.exp(own - top)
        total = jnp.sum(expo, axis=1, keepdims=True) + own_expo
        weights = expo.astype(BF16)
        copies[group][1].wait()
        accum = jnp.concatenate(
            [
                jnp.dot(
                    weights[row * 8 : (row + 1) * 8],
                    v_ref[first + row, 0],
                    preferred_element_type=F32,
                )
                for row in range(rows)
            ]
        )
        accum = accum + own_expo.astype(BF16).astype(F32) * spread(own_v)
        held[first * 8 : (first + rows) * 8, :] = accum / total

    for h in range(8):
        piece = held[pl.ds(h, 16, stride=8), :].astype(BF16)
        for there in range(16):
            out_ref[there, :, h * 128 : (h + 1) * 128] = piece
    mix_copy.wait()


def attend(q, k, v, own_k, own_v, counts, skip, mix):
    vmem, anywhere = pl.BlockSpec(), pl.BlockSpec(memory_space=pl.ANY)
    own_k, own_v = own_k.reshape(16, 128), own_v.reshape(16, 128)
    return pl.pallas_call(
        attend_body,
        in_specs=[
            pl.BlockSpec(memory_space=pltpu.SMEM),
            vmem,
            anywhere,
            anywhere,
            vmem,
            vmem,
            vmem,
            anywhere,
        ],
        out_shape=[
            jax.ShapeDtypeStruct((16, 16, 1280), BF16),
            pltpu.VMEM((1024, 256), BF16),
        ],
        scratch_shapes=[
            pltpu.VMEM((16, 1, 512, 128), BF16),
            pltpu.VMEM((16, 1, 512, 128), BF16),
            pltpu.VMEM((16, 128), F32),
            pltpu.VMEM((16, 128), F32),
            pltpu.VMEM((128, 128), F32),
            pltpu.SemaphoreType.DMA((8,)),
            pltpu.SemaphoreType.DMA,
        ],
        compiler_params=pltpu.CompilerParams(vmem_limit_bytes=LIMIT),
    )(counts, *[in_hbm(value) for value in (q, k, v, own_k, own_v, skip, mix)])


def project_body(got_ref, own_ref, peer_ref, gain_ref, out_ref):
    attn = got_ref[:, :1024]
    skip = got_ref[:, 1024:].astype(F32)
    x, c, t, _ = place()
    for side, mix_ref in enumerate((own_ref, peer_ref)):
        part = jnp.dot(attn, mix_ref[...], preferred_element_type=F32)
        holds = t == 2 * x + (c if side == 0 else 1 - c)
        part = jnp.where(holds, part + skip, part).astype(BF16)
        for j in range(2):
            cols = part[:, j * 128 : (j + 1) * 128].reshape(8, 32, 128)
            out_ref[:, (2 * side + j) * 32 : (2 * side + j + 1) * 32, :] = cols
    gain = gain_ref[...]
    for there in range(8):
        out_ref[there, 128:, :] = gain


def project(got, mix_own, mix_peer, gain):
    return pl.pallas_call(
        project_body,
        out_shape=jax.ShapeDtypeStruct((8, 136, 128), BF16),
        compiler_params=pltpu.CompilerParams(vmem_limit_bytes=LIMIT),
    )(got, mix_own, mix_peer, gain)


def total_body(got_ref, out_ref, gain_ref):
    total = got_ref[0, :128, :].astype(F32)
    for source in range(1, 8):
        total += got_ref[source, :128, :].astype(F32)
    total = total.astype(BF16)
    for there in range(8):
        out_ref[there] = total
    for there in range(8):
        gain_ref[there * 8 : (there + 1) * 8, :] = got_ref[there, 128:, :].astype(F32)


def total_call(got):
    return pl.pallas_call(
        total_body,
        out_shape=[
            jax.ShapeDtypeStruct((8, 128, 128), BF16),
            jax.ShapeDtypeStruct((64, 128), F32),
        ],
        compiler_params=pltpu.CompilerParams(vmem_limit_bytes=LIMIT),
    )(got)


def turn(shift):
    pairs = []
    for x in range(4):
        for c in range(2):
            for y in range(4):
                here = (x * 2 + c) * 4 + y
                if c == 0:
                    there = (((x + shift) % 4) * 2 + c) * 4 + y
                else:
                    there = (x * 2 + c) * 4 + (y + shift) % 4
                pairs.append((here, there))
    return pairs


def turn_other(shift):
    pairs = []
    for x in range(4):
        for c in range(2):
            for y in range(4):
                here = (x * 2 + c) * 4 + y
                if c == 1:
                    there = (((x + shift) % 4) * 2 + c) * 4 + y
                else:
                    there = (x * 2 + c) * 4 + (y + shift) % 4
                pairs.append((here, there))
    return pairs


def swap_core(value):
    return lax.ppermute(value, "core", [(0, 1), (1, 0)])


def rows_of(column, copies):
    wide = jnp.broadcast_to(column, (256, 128))
    return [jnp.transpose(wide[h * 128 : (h + 1) * 128])[:1] for h in range(2)]


def fetch(lexicons, at, count, target, sems):
    copies = []
    for i in range(count):
        group = []
        for half in range(2):
            row = pl.multiple_of(number(*BLOCKS[at + i], half) * 256, 256)
            for side, lex in enumerate(lexicons):
                copy = pltpu.make_async_copy(
                    lex.at[pl.ds(row, 256), :],
                    target.at[side, pl.ds(i * 512 + half * 256, 256), :],
                    sems.at[4 * i + 2 * half + side],
                )
                copy.start()
                group.append(copy)
        copies.append(group)
    return copies


def head_body(plan, *refs):
    sides, at, ready, following, first, last = plan
    refs = list(refs)
    take = lambda n: [refs.pop(0) for _ in range(n)]
    total = sum(sides)
    sources = take(len(sides))
    gain, *lexicons = take(3)
    if not first:
        z_in, sq_in = take(2)
    if ready:
        (lexs,) = take(1)
    if last:
        sharp_ref, chosen_ref = take(2)
        z_out, pick_out, lse_out, tok_out = take(4)
    else:
        z_out, pick_out, sq_out = take(3)
    if following:
        (lex_next,) = take(1)
    if first:
        for source, copy_out in zip(sources, take(len(sources))):
            copy_out[...] = source[...]
    copies = None
    if not ready:
        lexs, sems = take(2)
        copies = fetch(lexicons, at, total, lexs, sems)
    if following:
        next_copies = fetch(lexicons, at + total, following, lex_next, *take(1))
    xs, held = take(2)
    x, c, t, y = place()
    mine = x * 4 + y
    squares = None if first else sq_in[...]
    own_piece, own_part = mine // 2, pl.multiple_of((mine % 2) * 16, 16)
    places = [(source, side) for source, some in zip(sources, sides) for side in range(some)]
    for start in range(0, total, 2):
        pair = range(start, min(start + 2, total))
        for i in pair:
            source, side = places[i]
            pick_out[i] = source[side, own_piece, :, pl.ds(own_part, 16), :]
            for j in range(4):
                wide = source[side, :, j].astype(F32).reshape(256, 128)
                squares = wide * wide if squares is None else squares + wide * wide
                row = gain[pl.ds(number(*BLOCKS[at + i], j // 2) * 2 + j % 2, 1), :]
                xs[:, i * 512 + j * 128 : i * 512 + (j + 1) * 128] = (wide * row).astype(BF16)
        if copies is not None:
            for i in pair:
                for copy in copies[i]:
                    copy.wait()
        span = slice(start * 512, (pair[-1] + 1) * 512)
        for side in range(2):
            cols = slice(side * 512, (side + 1) * 512)
            part = jnp.dot(xs[:, span], lexs[side, span, :], preferred_element_type=F32)
            if start:
                z_out[:, cols] += part
            elif first:
                z_out[:, cols] = part
            else:
                z_out[:, cols] = z_in[:, cols] + part
    if not last:
        sq_out[...] = squares
    if following:
        for group in next_copies:
            for copy in group:
                copy.wait()
    if last:
        sharp = column_of(sharp_ref[...], held)
        chosen = column_of(chosen_ref[...].astype(F32), held).astype(jnp.int32)
        scale = lax.rsqrt(jnp.sum(squares, axis=1, keepdims=True) / 8192.0 + 1e-05) * sharp
        z = z_out[...] * scale
        z_out[...] = z
        top = jnp.max(z, axis=1, keepdims=True)
        lse = top + jnp.log(jnp.sum(jnp.exp(z - top), axis=1, keepdims=True))
        token = jnp.zeros((256, 1), F32)
        for side in range(2):
            base = (((x * 2 + (c if side == 0 else 1 - c)) * 8 + t) * 4 + y) * 512
            here = lax.broadcasted_iota(jnp.int32, (256, 512), 1) == chosen - base
            part = jnp.where(here, z[:, side * 512 : (side + 1) * 512], 0.0)
            token += jnp.sum(part, axis=1, keepdims=True)
        odd = lax.broadcasted_iota(jnp.int32, (256, 128), 0) % 2
        low, high = rows_of(lse, 256)
        lse_out[...] = jnp.where(odd == 0, low, high)
        low, high = rows_of(token, 256)
        tok_out[0:1, :] = low
        tok_out[1:2, :] = high


def head_call(sources, at, following, gain, lex_own, lex_peer, state, lexs, closing):
    sides = [source.shape[0] for source in sources]
    total = sum(sides)
    first, ready, last = state is None, lexs is not None, closing is not None
    vmem, anywhere = pl.BlockSpec(), pl.BlockSpec(memory_space=pl.ANY)
    in_specs = [vmem] * (len(sources) + 1) + [anywhere] * 2
    operands = [*sources, gain, in_hbm(lex_own), in_hbm(lex_peer)]
    for extra in (state, lexs, closing):
        if extra is not None:
            operands += list(extra)
            in_specs += [vmem] * len(extra)
    out_shape = [
        jax.ShapeDtypeStruct((256, 1024), F32),
        jax.ShapeDtypeStruct((total, 4, 16, 128), BF16),
    ]
    scratch = []
    if last:
        out_shape += [
            jax.ShapeDtypeStruct((256, 128), F32),
            jax.ShapeDtypeStruct((2, 128), F32),
        ]
    else:
        out_shape += [jax.ShapeDtypeStruct((256, 128), F32)]
    if following:
        out_shape += [pltpu.VMEM((2, 512 * following, 512), BF16)]
    if first:
        out_shape += [jax.ShapeDtypeStruct(source.shape, source.dtype) for source in sources]
    if not ready:
        scratch += [pltpu.VMEM((2, 512 * total, 512), BF16), pltpu.SemaphoreType.DMA((4 * total,))]
    if following:
        scratch += [pltpu.SemaphoreType.DMA((4 * following,))]
    scratch += [pltpu.VMEM((256, 512 * total), BF16), pltpu.VMEM((128, 128), F32)]
    return pl.pallas_call(
        functools.partial(head_body, (sides, at, ready, following, first, last)),
        in_specs=in_specs,
        out_shape=out_shape,
        scratch_shapes=scratch,
        compiler_params=pltpu.CompilerParams(vmem_limit_bytes=LIMIT),
        cost_estimate=pl.CostEstimate(
            flops=2 * 256 * 512 * 1024 * total,
            bytes_accessed=total * (2**20 + 2**18) + 2**21,
            transcendentals=0,
        ),
    )(*operands)


def pile_body(first_ref, second_ref, out_ref):
    out_ref[0] = first_ref[...]
    out_ref[1] = second_ref[...]


def pile(first, second):
    return pl.pallas_call(
        pile_body,
        out_shape=jax.ShapeDtypeStruct((2, 8, 4, 32, 128), BF16),
        compiler_params=pltpu.CompilerParams(vmem_limit_bytes=LIMIT),
        cost_estimate=pl.CostEstimate(flops=0, bytes_accessed=2**20, transcendentals=0),
    )(first, second)


def mass_body(z_ref, lse_ref, tok_ref, level_ref, *refs):
    picks, (out_ref, norm_out, hidden_out, heap, held) = refs[:-5], refs[-5:]
    at = 0
    for pick in picks:
        heap[at : at + pick.shape[0]] = pick[...]
        at += pick.shape[0]
    x, c, t, y = place()
    spots = [(far % 4, side % 4) for far, side in BLOCKS]
    for yb in range(4):
        dx, dy = (t // 2 - x + 4) % 4, (yb - y + 4) % 4
        far, side = jnp.where(c == 0, dx, dy), jnp.where(c == 0, dy, dx)
        spot = jnp.int32(0)
        for i, (f, s) in enumerate(spots):
            spot = jnp.where((far == f) & (side == s), i, spot)
        piece = heap[spot]
        for j in range(2):
            cols = slice(yb * 256 + j * 128, yb * 256 + (j + 1) * 128)
            hidden_out[:, cols] = jnp.where(t % 2 == c, piece[j], piece[2 + j])
    level = column_of(level_ref[...], held)
    parts = lse_ref[...]
    odd = lax.broadcasted_iota(jnp.int32, parts.shape, 0) % 2
    columns = []
    for h in range(2):
        top = jnp.max(jnp.where(odd == h, parts, -jnp.inf), axis=0, keepdims=True)
        total = jnp.sum(jnp.where(odd == h, jnp.exp(parts - top), 0.0), axis=0, keepdims=True)
        norm = top + jnp.log(total)
        norm_out[h : h + 1, :] = norm
        columns.append(jnp.transpose(jnp.broadcast_to(norm, (128, 128)))[:, :1])
    logp = z_ref[...] - jnp.concatenate(columns, axis=0)
    gate = cut_slope * (level + logp * (1.0 / LN2))
    kept = jnp.sum(jnp.exp(logp) / (1.0 + jnp.exp(-gate)), axis=1, keepdims=True)
    low, high = rows_of(kept, 512)
    which = lax.broadcasted_iota(jnp.int32, (512, 128), 0) % 4
    out_ref[...] = jnp.where(
        which == 0,
        low,
        jnp.where(which == 1, high, jnp.where(which == 2, tok_ref[0:1, :], tok_ref[1:2, :])),
    )


def mass_call(z, lse, tok, level, picks):
    return pl.pallas_call(
        mass_body,
        out_shape=[
            jax.ShapeDtypeStruct((512, 128), F32),
            jax.ShapeDtypeStruct((2, 128), F32),
            jax.ShapeDtypeStruct((16, 1024), BF16),
        ],
        scratch_shapes=[pltpu.VMEM((16, 4, 16, 128), BF16), pltpu.VMEM((128, 128), F32)],
        compiler_params=pltpu.CompilerParams(vmem_limit_bytes=LIMIT),
    )(z, lse, tok, level, *picks)


def shards(
    probe_vectors,
    stored_lookup_vectors,
    stored_content_vectors,
    fresh_lookup_vector,
    fresh_content_vector,
    history_counts,
    mixing_matrix,
    skip_stream,
    closing_multiplier,
    lexicon_matrix,
    sharpening_factor,
    desired_perplexity,
    chosen_symbols,
):
    mix_peer = swap_core(mixing_matrix)
    lex_peer = swap_core(lexicon_matrix)

    sent, mix_own = attend(
        probe_vectors,
        stored_lookup_vectors,
        stored_content_vectors,
        fresh_lookup_vector,
        fresh_content_vector,
        history_counts,
        skip_stream,
        mixing_matrix,
    )
    got = lax.all_to_all(sent, ("x", "rep"), 0, 0, tiled=True).reshape(256, 1280)
    gain_rows = closing_multiplier.reshape(8, 128)
    sent = project(got, mix_own, mix_peer, gain_rows)
    got = lax.all_to_all(sent, "tensor", 0, 0, tiled=True)
    sent, gain = total_call(got)

    own = lax.all_to_all(sent, "tensor", 0, 0, tiled=True).reshape(8, 4, 32, 128)
    side = lambda v, s: lax.ppermute(v, PLANE, turn_other(s))
    far = lambda v, s: lax.ppermute(v, PLANE, turn(s))
    low = pile(own, side(own, 1))
    high = pile(side(own, -1), side(own, 2))
    left_low, right_high = far(low, 1), far(high, -1)
    past_low, past_high = far(left_low, 1), far(right_high, -1)

    fixed = (gain, lexicon_matrix, lex_peer)
    z, pick_0, sq, low, high = head_call([low, high], 0, 0, *fixed, None, None, None)
    left_high, right_low = far(high, 1), far(low, -1)
    z, pick_1, sq = head_call([left_low, right_high], 4, 0, *fixed, (z, sq), None, None)
    z, pick_2, sq, lexs = head_call([left_high, right_low], 8, 4, *fixed, (z, sq), None, None)
    closing = (sharpening_factor.reshape(4, 128), chosen_symbols.reshape(4, 128))
    z, pick_3, lse, tok = head_call(
        [past_low, past_high], 12, 0, *fixed, (z, sq), (lexs,), closing
    )
    picked = [pick_0, pick_1, pick_2, pick_3]
    every_lse = lax.all_to_all(lse.reshape(128, 2, 128), SAME_CORE, 0, 0, tiled=True)
    levels = desired_perplexity.reshape(4, 128)
    sent, norm, hidden = mass_call(z, every_lse.reshape(256, 128), tok, levels, picked)
    got = lax.all_to_all(sent.reshape(128, 4, 128), SAME_CORE, 0, 0, tiled=True)
    kept, tok = jnp.sum(got, axis=0).reshape(2, 256)
    token_logp = tok - norm.reshape(256)
    c = lax.axis_index("core")
    level = lax.dynamic_index_in_dim(desired_perplexity.reshape(4, 2, 64), c, 1, keepdims=False)
    level = level.reshape(256)
    token_logw = token_logp + jax.nn.log_sigmoid(cut_slope * (level + token_logp / LN2))
    mine_out = -(token_logw - jnp.log(kept)) / LN2
    peer_out = swap_core(mine_out)
    even = jnp.where(c == 0, mine_out, peer_out).reshape(4, 64)
    odd = jnp.where(c == 0, peer_out, mine_out).reshape(4, 64)
    surprise = jnp.stack([even, odd], axis=1).reshape(512)
    next_targets = desired_perplexity - 0.1 * (surprise - 5.0)
    return (hidden, next_targets, surprise)


def solution(mesh):
    fine = Mesh(mesh.devices.reshape(4, 2, 8, 4), ("x", "core", "tensor", "rep"))
    rows = ("x", "core", "rep")
    placed = (
        P(rows, "tensor", None),
        P(rows, "tensor", None, None),
        P(rows, "tensor", None, None),
        P(rows, "tensor", None),
        P(rows, "tensor", None),
        P(rows),
        P("tensor", rows),
        P(rows, "tensor"),
        P("tensor"),
        P(None, ("x", "core", "tensor", "rep")),
        P(),
        P(),
        P(),
    )
    return jax.shard_map(
        shards,
        mesh=fine,
        in_specs=placed,
        out_specs=(P(rows, "tensor"), P(), P()),
        check_vma=False,
    )
```

```python
import functools
import math

import jax
import jax.numpy as jnp
from jax import lax
from jax.experimental import pallas as pl
from jax.experimental.pallas import tpu as pltpu
from jax.sharding import Mesh
from jax.sharding import PartitionSpec as P

cut_slope = 4.0
LN2 = math.log(2.0)
F32 = jnp.float32
BF16 = jnp.bfloat16
PLANE = ("x", "core", "rep")
EVERY = ("x", "core", "tensor", "rep")
SAME_CORE = ("x", "tensor", "rep")
LIMIT = 16 * 1024 * 1024


def place():
    return tuple(lax.axis_index(name) for name in ("x", "core", "tensor", "rep"))


def number(far, side, half):
    x, c, _, y = place()
    even = c == 0
    bx = jnp.where(even, x + (far % 4), x + (side % 4)) % 4
    by = jnp.where(even, y + (side % 4), y + (far % 4)) % 4
    return (bx * 2 + (c if half == 0 else 1 - c)) * 4 + by


def column_of(table, held):
    c = lax.axis_index("core")
    held[...] = jnp.transpose(jnp.concatenate([table, jnp.zeros((124, 128), F32)]))
    start = pl.multiple_of(c * 64, 64)
    return jnp.concatenate([held[pl.ds(start, 64), i : i + 1] for i in range(4)])


LOWS, HIGHS = (0, 1), (-1, 2)
BLOCKS = [
    (far, side)
    for far, sides in (
        (0, LOWS),
        (0, HIGHS),
        (-1, LOWS),
        (1, HIGHS),
        (-1, HIGHS),
        (1, LOWS),
        (2, LOWS),
        (2, HIGHS),
    )
    for side in sides
]


def in_hbm(value):
    return pltpu.with_memory_space_constraint(value, pltpu.HBM)


def in_vmem(value):
    return pltpu.with_memory_space_constraint(value, pltpu.VMEM)


def attend_body(
    counts, q_ref, k_hbm, v_hbm, own_k_ref, own_v_ref, skip_ref, mix, out_ref, mix_out, *scratch
):
    k_ref, v_ref, own_k, own_v, held, sems, mix_sem = scratch
    rows = 4
    groups = k_ref.shape[0] // rows
    score_scale = 1.0 / math.sqrt(k_ref.shape[3])
    copies = []
    for group in range(groups):
        span = pl.ds(group * rows, rows)
        pair = [
            pltpu.make_async_copy(k_hbm.at[span], k_ref.at[span], sems.at[2 * group]),
            pltpu.make_async_copy(v_hbm.at[span], v_ref.at[span], sems.at[2 * group + 1]),
        ]
        for copy in pair:
            copy.start()
        copies.append(pair)
    mix_copy = pltpu.make_async_copy(mix, mix_out, mix_sem)
    mix_copy.start()
    own_k[...] = own_k_ref[...].astype(F32)
    own_v[...] = own_v_ref[...].astype(F32)
    for there in range(16):
        block = there % 4
        out_ref[there, :, 1024:] = skip_ref[:, block * 256 : (block + 1) * 256]

    for group in range(groups):
        first = group * rows
        spread = lambda ref: jnp.concatenate(
            [jnp.broadcast_to(ref[first + row : first + row + 1], (8, 128)) for row in range(rows)]
        )
        q = q_ref[first : first + rows].reshape(rows * 8, 128)
        own = score_scale * jnp.sum(q.astype(F32) * spread(own_k), axis=1, keepdims=True)
        copies[group][0].wait()
        scores = score_scale * jnp.concatenate(
            [
                lax.dot_general(
                    q_ref[first + row],
                    k_ref[first + row, 0],
                    (((1,), (1,)), ((), ())),
                    preferred_element_type=F32,
                )
                for row in range(rows)
            ]
        )
        position = lax.broadcasted_iota(jnp.int32, (8, scores.shape[1]), 1)
        live = jnp.concatenate([position < counts[first + row] for row in range(rows)])
        top = jnp.maximum(jnp.max(jnp.where(live, scores, -1e30), axis=1, keepdims=True), own)
        expo = jnp.where(live, jnp.exp(scores - top), 0.0)
        own_expo = jnp.exp(own - top)
        total = jnp.sum(expo, axis=1, keepdims=True) + own_expo
        weights = expo.astype(BF16)
        copies[group][1].wait()
        accum = jnp.concatenate(
            [
                jnp.dot(
                    weights[row * 8 : (row + 1) * 8],
                    v_ref[first + row, 0],
                    preferred_element_type=F32,
                )
                for row in range(rows)
            ]
        )
        accum = accum + own_expo.astype(BF16).astype(F32) * spread(own_v)
        held[first * 8 : (first + rows) * 8, :] = accum / total

    for h in range(8):
        piece = held[pl.ds(h, 16, stride=8), :].astype(BF16)
        for there in range(16):
            out_ref[there, :, h * 128 : (h + 1) * 128] = piece
    mix_copy.wait()


def attend(q, k, v, own_k, own_v, counts, skip, mix):
    vmem, anywhere = pl.BlockSpec(), pl.BlockSpec(memory_space=pl.ANY)
    own_k, own_v = own_k.reshape(16, 128), own_v.reshape(16, 128)
    return pl.pallas_call(
        attend_body,
        in_specs=[
            pl.BlockSpec(memory_space=pltpu.SMEM),
            vmem,
            anywhere,
            anywhere,
            vmem,
            vmem,
            vmem,
            anywhere,
        ],
        out_shape=[
            jax.ShapeDtypeStruct((16, 16, 1280), BF16),
            pltpu.VMEM((1024, 256), BF16),
        ],
        scratch_shapes=[
            pltpu.VMEM((16, 1, 512, 128), BF16),
            pltpu.VMEM((16, 1, 512, 128), BF16),
            pltpu.VMEM((16, 128), F32),
            pltpu.VMEM((16, 128), F32),
            pltpu.VMEM((128, 128), F32),
            pltpu.SemaphoreType.DMA((8,)),
            pltpu.SemaphoreType.DMA,
        ],
        compiler_params=pltpu.CompilerParams(vmem_limit_bytes=LIMIT),
    )(*[in_hbm(value) for value in (counts, q, k, v, own_k, own_v, skip, mix)])


def project_body(got_ref, own_ref, peer_ref, gain_ref, out_ref):
    attn = got_ref[:, :1024]
    skip = got_ref[:, 1024:].astype(F32)
    x, c, t, _ = place()
    for side, mix_ref in enumerate((own_ref, peer_ref)):
        part = jnp.dot(attn, mix_ref[...], preferred_element_type=F32)
        holds = t == 2 * x + (c if side == 0 else 1 - c)
        part = jnp.where(holds, part + skip, part).astype(BF16)
        for j in range(2):
            cols = part[:, j * 128 : (j + 1) * 128].reshape(8, 32, 128)
            out_ref[:, (2 * side + j) * 32 : (2 * side + j + 1) * 32, :] = cols
    gain = gain_ref[...]
    for there in range(8):
        out_ref[there, 128:, :] = gain


def project(got, mix_own, mix_peer, gain):
    return pl.pallas_call(
        project_body,
        out_shape=jax.ShapeDtypeStruct((8, 136, 128), BF16),
        compiler_params=pltpu.CompilerParams(vmem_limit_bytes=LIMIT),
    )(got, mix_own, mix_peer, gain)


def total_body(got_ref, out_ref, gain_ref):
    total = got_ref[0, :128, :].astype(F32)
    for source in range(1, 8):
        total += got_ref[source, :128, :].astype(F32)
    total = total.astype(BF16)
    for there in range(8):
        out_ref[there] = total
    for there in range(8):
        gain_ref[there * 8 : (there + 1) * 8, :] = got_ref[there, 128:, :].astype(F32)


def total_call(got):
    return pl.pallas_call(
        total_body,
        out_shape=[
            jax.ShapeDtypeStruct((8, 128, 128), BF16),
            jax.ShapeDtypeStruct((64, 128), F32),
        ],
        compiler_params=pltpu.CompilerParams(vmem_limit_bytes=LIMIT),
    )(got)


def turn(shift):
    pairs = []
    for x in range(4):
        for c in range(2):
            for y in range(4):
                here = (x * 2 + c) * 4 + y
                if c == 0:
                    there = (((x + shift) % 4) * 2 + c) * 4 + y
                else:
                    there = (x * 2 + c) * 4 + (y + shift) % 4
                pairs.append((here, there))
    return pairs


def turn_other(shift):
    pairs = []
    for x in range(4):
        for c in range(2):
            for y in range(4):
                here = (x * 2 + c) * 4 + y
                if c == 1:
                    there = (((x + shift) % 4) * 2 + c) * 4 + y
                else:
                    there = (x * 2 + c) * 4 + (y + shift) % 4
                pairs.append((here, there))
    return pairs


def swap_core(value):
    return lax.ppermute(value, "core", [(0, 1), (1, 0)])


def rows_of(column, copies):
    wide = jnp.broadcast_to(column, (256, 128))
    return [jnp.transpose(wide[h * 128 : (h + 1) * 128])[:1] for h in range(2)]


def fetch(lexicon, at, count, target, sems):
    copies = []
    for i in range(count):
        group = []
        for half in range(2):
            row = pl.multiple_of(number(*BLOCKS[at + i], half) * 256, 256)
            copy = pltpu.make_async_copy(
                lexicon.at[pl.ds(row, 256), :],
                target.at[pl.ds(i * 512 + half * 256, 256), :],
                sems.at[2 * i + half],
            )
            copy.start()
            group.append(copy)
        copies.append(group)
    return copies


def head_body(plan, *refs):
    sides, at, ready, following, first, last = plan
    refs = list(refs)
    take = lambda n: [refs.pop(0) for _ in range(n)]
    total = sum(sides)
    sources = take(len(sides))
    gain, lex_own, lex_peer = take(3)
    if not first:
        z_in, sq_in = take(2)
    if ready:
        (lexs,) = take(1)
    if last:
        sharp_ref, chosen_ref = take(2)
        z_out, pick_out, lse_out, tok_out = take(4)
    else:
        z_out, pick_out, sq_out = take(3)
    if following:
        (lex_next,) = take(1)
    if first:
        for source, copy_out in zip(sources, take(len(sources))):
            copy_out[...] = source[...]
    copies = None
    if not ready:
        lexs, sems = take(2)
        copies = fetch(lex_own, at, total, lexs, sems)
    if following:
        next_copies = fetch(lex_own, at + total, following, lex_next, *take(1))
    xs, held = take(2)
    x, c, t, y = place()
    mine = x * 4 + y
    squares = None if first else sq_in[...]
    own_piece, own_part = mine // 2, pl.multiple_of((mine % 2) * 16, 16)
    places = [(source, side) for source, some in zip(sources, sides) for side in range(some)]
    for start in range(0, total, 2):
        pair = range(start, min(start + 2, total))
        for i in pair:
            source, side = places[i]
            pick_out[i] = source[side, own_piece, :, pl.ds(own_part, 16), :]
            for j in range(4):
                wide = source[side, :, j].astype(F32).reshape(256, 128)
                squares = wide * wide if squares is None else squares + wide * wide
                row = gain[pl.ds(number(*BLOCKS[at + i], j // 2) * 2 + j % 2, 1), :]
                xs[:, i * 512 + j * 128 : i * 512 + (j + 1) * 128] = (wide * row).astype(BF16)
        if copies is not None:
            for i in pair:
                for copy in copies[i]:
                    copy.wait()
        span = slice(start * 512, (pair[-1] + 1) * 512)
        for side in range(2):
            cols = slice(side * 512, (side + 1) * 512)
            if side == 0:
                part = jnp.dot(xs[:, span], lexs[span, :], preferred_element_type=F32)
            else:
                part = 0.0
                for i in pair:
                    for half in range(2):
                        row = pl.multiple_of(number(*BLOCKS[at + i], half) * 256, 256)
                        x_cols = slice(i * 512 + half * 256, i * 512 + (half + 1) * 256)
                        part += jnp.dot(
                            xs[:, x_cols], lex_peer[pl.ds(row, 256), :], preferred_element_type=F32
                        )
            if start:
                z_out[:, cols] += part
            elif first:
                z_out[:, cols] = part
            else:
                z_out[:, cols] = z_in[:, cols] + part
    if not last:
        sq_out[...] = squares
    if following:
        for group in next_copies:
            for copy in group:
                copy.wait()
    if last:
        sharp = column_of(sharp_ref[...], held)
        chosen = column_of(chosen_ref[...].astype(F32), held).astype(jnp.int32)
        scale = lax.rsqrt(jnp.sum(squares, axis=1, keepdims=True) / 8192.0 + 1e-05) * sharp
        z = z_out[...] * scale
        z_out[...] = z
        top = jnp.max(z, axis=1, keepdims=True)
        lse = top + jnp.log(jnp.sum(jnp.exp(z - top), axis=1, keepdims=True))
        token = jnp.zeros((256, 1), F32)
        for side in range(2):
            base = (((x * 2 + (c if side == 0 else 1 - c)) * 8 + t) * 4 + y) * 512
            here = lax.broadcasted_iota(jnp.int32, (256, 512), 1) == chosen - base
            part = jnp.where(here, z[:, side * 512 : (side + 1) * 512], 0.0)
            token += jnp.sum(part, axis=1, keepdims=True)
        odd = lax.broadcasted_iota(jnp.int32, (256, 128), 0) % 2
        low, high = rows_of(lse, 256)
        lse_out[...] = jnp.where(odd == 0, low, high)
        low, high = rows_of(token, 256)
        tok_out[0:1, :] = low
        tok_out[1:2, :] = high


def head_call(sources, at, following, gain, lex_own, lex_peer, state, lexs, closing):
    sides = [source.shape[0] for source in sources]
    total = sum(sides)
    first, ready, last = state is None, lexs is not None, closing is not None
    vmem, anywhere = pl.BlockSpec(), pl.BlockSpec(memory_space=pl.ANY)
    in_specs = [vmem] * (len(sources) + 1) + [anywhere, vmem]
    operands = [*sources, gain, in_hbm(lex_own), in_vmem(lex_peer)]
    for extra in (state, lexs, closing):
        if extra is not None:
            operands += list(extra)
            in_specs += [vmem] * len(extra)
    out_shape = [
        jax.ShapeDtypeStruct((256, 1024), F32),
        jax.ShapeDtypeStruct((total, 4, 16, 128), BF16),
    ]
    scratch = []
    if last:
        out_shape += [
            jax.ShapeDtypeStruct((256, 128), F32),
            jax.ShapeDtypeStruct((2, 128), F32),
        ]
    else:
        out_shape += [jax.ShapeDtypeStruct((256, 128), F32)]
    if following:
        out_shape += [pltpu.VMEM((512 * following, 512), BF16)]
    if first:
        out_shape += [jax.ShapeDtypeStruct(source.shape, source.dtype) for source in sources]
    if not ready:
        scratch += [pltpu.VMEM((512 * total, 512), BF16), pltpu.SemaphoreType.DMA((2 * total,))]
    if following:
        scratch += [pltpu.SemaphoreType.DMA((2 * following,))]
    scratch += [pltpu.VMEM((256, 512 * total), BF16), pltpu.VMEM((128, 128), F32)]
    return pl.pallas_call(
        functools.partial(head_body, (sides, at, ready, following, first, last)),
        in_specs=in_specs,
        out_shape=out_shape,
        scratch_shapes=scratch,
        compiler_params=pltpu.CompilerParams(vmem_limit_bytes=LIMIT),
        cost_estimate=pl.CostEstimate(
            flops=2 * 256 * 512 * 1024 * total,
            bytes_accessed=total * (2**20 + 2**18) + 2**21,
            transcendentals=0,
        ),
    )(*operands)


def pile_body(first_ref, second_ref, out_ref):
    out_ref[0] = first_ref[...]
    out_ref[1] = second_ref[...]


def pile(first, second):
    return pl.pallas_call(
        pile_body,
        out_shape=jax.ShapeDtypeStruct((2, 8, 4, 32, 128), BF16),
        compiler_params=pltpu.CompilerParams(vmem_limit_bytes=LIMIT),
        cost_estimate=pl.CostEstimate(flops=0, bytes_accessed=2**20, transcendentals=0),
    )(first, second)


def mass_body(z_ref, lse_ref, tok_ref, level_ref, *refs):
    picks, (out_ref, norm_out, hidden_out, heap, held) = refs[:-5], refs[-5:]
    at = 0
    for pick in picks:
        heap[at : at + pick.shape[0]] = pick[...]
        at += pick.shape[0]
    x, c, t, y = place()
    spots = [(far % 4, side % 4) for far, side in BLOCKS]
    for yb in range(4):
        dx, dy = (t // 2 - x + 4) % 4, (yb - y + 4) % 4
        far, side = jnp.where(c == 0, dx, dy), jnp.where(c == 0, dy, dx)
        spot = jnp.int32(0)
        for i, (f, s) in enumerate(spots):
            spot = jnp.where((far == f) & (side == s), i, spot)
        piece = heap[spot]
        for j in range(2):
            cols = slice(yb * 256 + j * 128, yb * 256 + (j + 1) * 128)
            hidden_out[:, cols] = jnp.where(t % 2 == c, piece[j], piece[2 + j])
    level = column_of(level_ref[...], held)
    parts = lse_ref[...]
    odd = lax.broadcasted_iota(jnp.int32, parts.shape, 0) % 2
    columns = []
    for h in range(2):
        top = jnp.max(jnp.where(odd == h, parts, -jnp.inf), axis=0, keepdims=True)
        total = jnp.sum(jnp.where(odd == h, jnp.exp(parts - top), 0.0), axis=0, keepdims=True)
        norm = top + jnp.log(total)
        norm_out[h : h + 1, :] = norm
        columns.append(jnp.transpose(jnp.broadcast_to(norm, (128, 128)))[:, :1])
    logp = z_ref[...] - jnp.concatenate(columns, axis=0)
    gate = cut_slope * (level + logp * (1.0 / LN2))
    kept = jnp.sum(jnp.exp(logp) / (1.0 + jnp.exp(-gate)), axis=1, keepdims=True)
    low, high = rows_of(kept, 512)
    which = lax.broadcasted_iota(jnp.int32, (512, 128), 0) % 4
    out_ref[...] = jnp.where(
        which == 0,
        low,
        jnp.where(which == 1, high, jnp.where(which == 2, tok_ref[0:1, :], tok_ref[1:2, :])),
    )


def mass_call(z, lse, tok, level, picks):
    return pl.pallas_call(
        mass_body,
        out_shape=[
            jax.ShapeDtypeStruct((512, 128), F32),
            jax.ShapeDtypeStruct((2, 128), F32),
            jax.ShapeDtypeStruct((16, 1024), BF16),
        ],
        scratch_shapes=[pltpu.VMEM((16, 4, 16, 128), BF16), pltpu.VMEM((128, 128), F32)],
        compiler_params=pltpu.CompilerParams(vmem_limit_bytes=LIMIT),
    )(z, lse, tok, level, *picks)


def swap_halves(rows):
    return jnp.concatenate([rows[:, 64:], rows[:, :64]], axis=1)


def surprise_body(got_ref, norm_ref, level_ref, out_ref):
    sums = jnp.sum(got_ref[...].reshape(64, 8, 128), axis=0)
    sums = sums[:4] + sums[4:]
    kept, token = sums[:2], sums[2:]
    table = level_ref[...]
    turned = swap_halves(table)
    even = lax.axis_index("core") == 0
    first, second = jnp.where(even, table, turned), jnp.where(even, turned, table)
    low = lax.broadcasted_iota(jnp.int32, (1, 128), 1) < 64
    level = jnp.concatenate(
        [jnp.where(low, first[2 * h : 2 * h + 1], second[2 * h + 1 : 2 * h + 2]) for h in range(2)]
    )
    token_logp = token - norm_ref[...]
    gate = cut_slope * (level + token_logp / LN2)
    log_gate = jnp.minimum(gate, 0.0) - jnp.log1p(jnp.exp(-jnp.abs(gate)))
    out_ref[...] = -(token_logp + log_gate - jnp.log(kept)) / LN2


def surprise_call(got, norm, level):
    return pl.pallas_call(
        surprise_body,
        out_shape=jax.ShapeDtypeStruct((2, 128), F32),
        compiler_params=pltpu.CompilerParams(vmem_limit_bytes=LIMIT),
    )(got, norm, level)


def merge_body(own_ref, peer_ref, level_ref, surprise_out, next_out):
    even = lax.axis_index("core") == 0
    own, peer = own_ref[...], peer_ref[...]
    evens, odds = jnp.where(even, own, peer), jnp.where(even, peer, own)
    low = lax.broadcasted_iota(jnp.int32, (1, 128), 1) < 64
    first = jnp.where(low, evens, swap_halves(odds))
    second = jnp.where(low, swap_halves(evens), odds)
    surprise = jnp.concatenate([first[:1], second[:1], first[1:], second[1:]])
    surprise_out[...] = surprise
    next_out[...] = level_ref[...] - 0.1 * (surprise - 5.0)


def merge_call(own, peer, level):
    return pl.pallas_call(
        merge_body,
        out_shape=[jax.ShapeDtypeStruct((4, 128), F32)] * 2,
        compiler_params=pltpu.CompilerParams(vmem_limit_bytes=LIMIT),
    )(own, peer, level)


def shards(
    probe_vectors,
    stored_lookup_vectors,
    stored_content_vectors,
    fresh_lookup_vector,
    fresh_content_vector,
    history_counts,
    mixing_matrix,
    skip_stream,
    closing_multiplier,
    lexicon_matrix,
    sharpening_factor,
    desired_perplexity,
    chosen_symbols,
):
    mix_peer = swap_core(mixing_matrix)

    sent, mix_own = attend(
        probe_vectors,
        stored_lookup_vectors,
        stored_content_vectors,
        fresh_lookup_vector,
        fresh_content_vector,
        history_counts,
        skip_stream,
        mixing_matrix,
    )
    lexicon_matrix, mix_peer, sent = lax.optimization_barrier((lexicon_matrix, mix_peer, sent))
    lex_peer = swap_core(lexicon_matrix)
    got = lax.all_to_all(sent, ("x", "rep"), 0, 0, tiled=True).reshape(256, 1280)
    gain_rows = closing_multiplier.reshape(8, 128)
    sent = project(got, mix_own, mix_peer, gain_rows)
    got = lax.all_to_all(sent, "tensor", 0, 0, tiled=True)
    sent, gain = total_call(got)

    own = lax.all_to_all(sent, "tensor", 0, 0, tiled=True).reshape(8, 4, 32, 128)
    side = lambda v, s: lax.ppermute(v, PLANE, turn_other(s))
    far = lambda v, s: lax.ppermute(v, PLANE, turn(s))
    ahead, behind, across = side(own, 1), side(own, -1), side(own, 2)
    low = pile(own, behind)
    ahead, across, low = lax.optimization_barrier((ahead, across, low))
    high = pile(ahead, across)
    left_low, right_high = far(low, 1), far(high, -1)
    past_low, past_high = far(left_low, 1), far(right_high, -1)

    fixed = (gain, lexicon_matrix, lex_peer)
    z, pick_0, sq, low, high = head_call([low, high], 0, 0, *fixed, None, None, None)
    left_high, right_low = far(high, 1), far(low, -1)
    z, pick_1, sq = head_call([left_low, right_high], 4, 0, *fixed, (z, sq), None, None)
    z, pick_2, sq, lexs = head_call([left_high, right_low], 8, 4, *fixed, (z, sq), None, None)
    closing = (sharpening_factor.reshape(4, 128), chosen_symbols.reshape(4, 128))
    z, pick_3, lse, tok = head_call(
        [past_low, past_high], 12, 0, *fixed, (z, sq), (lexs,), closing
    )
    picked = [pick_0, pick_1, pick_2, pick_3]
    every_lse = lax.all_to_all(lse.reshape(128, 2, 128), SAME_CORE, 0, 0, tiled=True)
    levels = desired_perplexity.reshape(4, 128)
    sent, norm, hidden = mass_call(z, every_lse.reshape(256, 128), tok, levels, picked)
    got = lax.all_to_all(sent.reshape(128, 4, 128), SAME_CORE, 0, 0, tiled=True)
    mine = surprise_call(got.reshape(512, 128), norm, levels)
    surprise, next_targets = merge_call(mine, swap_core(mine), levels)
    surprise, next_targets = surprise.reshape(512), next_targets.reshape(512)
    return (hidden, next_targets, surprise)


def solution(mesh):
    fine = Mesh(mesh.devices.reshape(4, 2, 8, 4), ("x", "core", "tensor", "rep"))
    rows = ("x", "core", "rep")
    placed = (
        P(rows, "tensor", None),
        P(rows, "tensor", None, None),
        P(rows, "tensor", None, None),
        P(rows, "tensor", None),
        P(rows, "tensor", None),
        P(rows),
        P("tensor", rows),
        P(rows, "tensor"),
        P("tensor"),
        P(None, ("x", "core", "tensor", "rep")),
        P(),
        P(),
        P(),
    )
    return jax.shard_map(
        shards,
        mesh=fine,
        in_specs=placed,
        out_specs=(P(rows, "tensor"), P(), P()),
        check_vma=False,
    )
```

```python
import functools
import math

import jax
import jax.numpy as jnp
from jax import lax
from jax.experimental import pallas as pl
from jax.experimental.pallas import tpu as pltpu
from jax.sharding import Mesh
from jax.sharding import PartitionSpec as P

cut_slope = 4.0
LN2 = math.log(2.0)
F32 = jnp.float32
BF16 = jnp.bfloat16
PLANE = ("x", "core", "rep")
EVERY = ("x", "core", "tensor", "rep")
SAME_CORE = ("x", "tensor", "rep")
LIMIT = 16 * 1024 * 1024


def place():
    return tuple(lax.axis_index(name) for name in ("x", "core", "tensor", "rep"))


def number(far, side, half):
    x, c, _, y = place()
    even = c == 0
    bx = jnp.where(even, x + (far % 4), x + (side % 4)) % 4
    by = jnp.where(even, y + (side % 4), y + (far % 4)) % 4
    return (bx * 2 + (c if half == 0 else 1 - c)) * 4 + by


def column_of(table, held):
    c = lax.axis_index("core")
    held[...] = jnp.transpose(jnp.concatenate([table, jnp.zeros((124, 128), F32)]))
    start = pl.multiple_of(c * 64, 64)
    return jnp.concatenate([held[pl.ds(start, 64), i : i + 1] for i in range(4)])


LOWS, HIGHS = (0, 1), (-1, 2)
BLOCKS = [
    (far, side)
    for far, sides in (
        (0, LOWS),
        (0, HIGHS),
        (-1, LOWS),
        (1, HIGHS),
        (-1, HIGHS),
        (1, LOWS),
        (2, LOWS),
        (2, HIGHS),
    )
    for side in sides
]


def in_hbm(value):
    return pltpu.with_memory_space_constraint(value, pltpu.HBM)


def in_vmem(value):
    return pltpu.with_memory_space_constraint(value, pltpu.VMEM)


def attend_body(
    counts, q_ref, k_hbm, v_hbm, own_k_ref, own_v_ref, skip_ref, mix, out_ref, mix_out, *scratch
):
    k_ref, v_ref, own_k, own_v, held, sems, mix_sem = scratch
    rows = 8
    groups = k_ref.shape[0] // rows
    score_scale = 1.0 / math.sqrt(k_ref.shape[3])
    copies = []
    for group in range(groups):
        span = pl.ds(group * rows, rows)
        pair = [
            pltpu.make_async_copy(k_hbm.at[span], k_ref.at[span], sems.at[2 * group]),
            pltpu.make_async_copy(v_hbm.at[span], v_ref.at[span], sems.at[2 * group + 1]),
        ]
        for copy in pair:
            copy.start()
        copies.append(pair)
    mix_copy = pltpu.make_async_copy(mix, mix_out, mix_sem)
    mix_copy.start()
    own_k[...] = own_k_ref[...].astype(F32)
    own_v[...] = own_v_ref[...].astype(F32)
    for there in range(16):
        block = there % 4
        out_ref[there, :, 1024:] = skip_ref[:, block * 256 : (block + 1) * 256]

    for group in range(groups):
        first = group * rows
        spread = lambda ref: jnp.concatenate(
            [jnp.broadcast_to(ref[first + row : first + row + 1], (8, 128)) for row in range(rows)]
        )
        q = q_ref[first : first + rows].reshape(rows * 8, 128)
        own = score_scale * jnp.sum(q.astype(F32) * spread(own_k), axis=1, keepdims=True)
        copies[group][0].wait()
        scores = score_scale * jnp.concatenate(
            [
                lax.dot_general(
                    q_ref[first + row],
                    k_ref[first + row, 0],
                    (((1,), (1,)), ((), ())),
                    preferred_element_type=F32,
                )
                for row in range(rows)
            ]
        )
        position = lax.broadcasted_iota(jnp.int32, (8, scores.shape[1]), 1)
        live = jnp.concatenate([position < counts[first + row] for row in range(rows)])
        top = jnp.maximum(jnp.max(jnp.where(live, scores, -1e30), axis=1, keepdims=True), own)
        expo = jnp.where(live, jnp.exp(scores - top), 0.0)
        own_expo = jnp.exp(own - top)
        total = jnp.sum(expo, axis=1, keepdims=True) + own_expo
        weights = expo.astype(BF16)
        copies[group][1].wait()
        accum = jnp.concatenate(
            [
                jnp.dot(
                    weights[row * 8 : (row + 1) * 8],
                    v_ref[first + row, 0],
                    preferred_element_type=F32,
                )
                for row in range(rows)
            ]
        )
        accum = accum + own_expo.astype(BF16).astype(F32) * spread(own_v)
        held[first * 8 : (first + rows) * 8, :] = accum / total

    for h in range(8):
        piece = held[pl.ds(h, 16, stride=8), :].astype(BF16)
        for there in range(16):
            out_ref[there, :, h * 128 : (h + 1) * 128] = piece
    mix_copy.wait()


def attend(q, k, v, own_k, own_v, counts, skip, mix):
    vmem, anywhere = pl.BlockSpec(), pl.BlockSpec(memory_space=pl.ANY)
    own_k, own_v = own_k.reshape(16, 128), own_v.reshape(16, 128)
    return pl.pallas_call(
        attend_body,
        in_specs=[
            pl.BlockSpec(memory_space=pltpu.SMEM),
            vmem,
            anywhere,
            anywhere,
            vmem,
            vmem,
            vmem,
            anywhere,
        ],
        out_shape=[
            jax.ShapeDtypeStruct((16, 16, 1280), BF16),
            pltpu.VMEM((1024, 256), BF16),
        ],
        scratch_shapes=[
            pltpu.VMEM((16, 1, 512, 128), BF16),
            pltpu.VMEM((16, 1, 512, 128), BF16),
            pltpu.VMEM((16, 128), F32),
            pltpu.VMEM((16, 128), F32),
            pltpu.VMEM((128, 128), F32),
            pltpu.SemaphoreType.DMA((8,)),
            pltpu.SemaphoreType.DMA,
        ],
        compiler_params=pltpu.CompilerParams(vmem_limit_bytes=LIMIT),
    )(*[in_hbm(value) for value in (counts, q, k, v, own_k, own_v, skip, mix)])


def project_body(got_ref, own_ref, peer_ref, gain_ref, out_ref):
    attn = got_ref[:, :1024]
    skip = got_ref[:, 1024:].astype(F32)
    x, c, t, _ = place()
    for side, mix_ref in enumerate((own_ref, peer_ref)):
        part = jnp.dot(attn, mix_ref[...], preferred_element_type=F32)
        holds = t == 2 * x + (c if side == 0 else 1 - c)
        part = jnp.where(holds, part + skip, part).astype(BF16)
        for j in range(2):
            cols = part[:, j * 128 : (j + 1) * 128].reshape(8, 32, 128)
            out_ref[:, (2 * side + j) * 32 : (2 * side + j + 1) * 32, :] = cols
    gain = gain_ref[...]
    for there in range(8):
        out_ref[there, 128:, :] = gain


def project(got, mix_own, mix_peer, gain):
    return pl.pallas_call(
        project_body,
        out_shape=jax.ShapeDtypeStruct((8, 136, 128), BF16),
        compiler_params=pltpu.CompilerParams(vmem_limit_bytes=LIMIT),
    )(got, mix_own, mix_peer, gain)


def total_body(got_ref, out_ref, gain_ref):
    total = got_ref[0, :128, :].astype(F32)
    for source in range(1, 8):
        total += got_ref[source, :128, :].astype(F32)
    total = total.astype(BF16)
    for there in range(8):
        out_ref[there] = total
    for there in range(8):
        gain_ref[there * 8 : (there + 1) * 8, :] = got_ref[there, 128:, :].astype(F32)


def total_call(got):
    return pl.pallas_call(
        total_body,
        out_shape=[
            jax.ShapeDtypeStruct((8, 128, 128), BF16),
            jax.ShapeDtypeStruct((64, 128), F32),
        ],
        compiler_params=pltpu.CompilerParams(vmem_limit_bytes=LIMIT),
    )(got)


def turn(shift):
    pairs = []
    for x in range(4):
        for c in range(2):
            for y in range(4):
                here = (x * 2 + c) * 4 + y
                if c == 0:
                    there = (((x + shift) % 4) * 2 + c) * 4 + y
                else:
                    there = (x * 2 + c) * 4 + (y + shift) % 4
                pairs.append((here, there))
    return pairs


def turn_other(shift):
    pairs = []
    for x in range(4):
        for c in range(2):
            for y in range(4):
                here = (x * 2 + c) * 4 + y
                if c == 1:
                    there = (((x + shift) % 4) * 2 + c) * 4 + y
                else:
                    there = (x * 2 + c) * 4 + (y + shift) % 4
                pairs.append((here, there))
    return pairs


def swap_core(value):
    return lax.ppermute(value, "core", [(0, 1), (1, 0)])


def rows_of(column, copies):
    wide = jnp.broadcast_to(column, (256, 128))
    return [jnp.transpose(wide[h * 128 : (h + 1) * 128])[:1] for h in range(2)]


def fetch(lexicon, at, count, target, sems):
    copies = []
    for i in range(count):
        group = []
        for half in range(2):
            row = pl.multiple_of(number(*BLOCKS[at + i], half) * 256, 256)
            copy = pltpu.make_async_copy(
                lexicon.at[pl.ds(row, 256), :],
                target.at[pl.ds(i * 512 + half * 256, 256), :],
                sems.at[2 * i + half],
            )
            copy.start()
            group.append(copy)
        copies.append(group)
    return copies


def head_body(plan, *refs):
    sides, at, ready, following, first, last = plan
    refs = list(refs)
    take = lambda n: [refs.pop(0) for _ in range(n)]
    total = sum(sides)
    sources = take(len(sides))
    gain, lex_own, lex_peer = take(3)
    if not first:
        z_in, sq_in = take(2)
    if ready:
        (lexs,) = take(1)
    if last:
        sharp_ref, chosen_ref = take(2)
        z_out, pick_out, lse_out, tok_out = take(4)
    else:
        z_out, pick_out, sq_out = take(3)
    if following:
        (lex_next,) = take(1)
    if first:
        for source, copy_out in zip(sources, take(len(sources))):
            copy_out[...] = source[...]
    copies = None
    if not ready:
        lexs, sems = take(2)
        copies = fetch(lex_own, at, total, lexs, sems)
    if following:
        next_copies = fetch(lex_own, at + total, following, lex_next, *take(1))
    xs, held = take(2)
    x, c, t, y = place()
    mine = x * 4 + y
    squares = None if first else sq_in[...]
    own_piece, own_part = mine // 2, pl.multiple_of((mine % 2) * 16, 16)
    places = [(source, side) for source, some in zip(sources, sides) for side in range(some)]
    for start in range(0, total, 2):
        pair = range(start, min(start + 2, total))
        for i in pair:
            source, side = places[i]
            pick_out[i] = source[side, own_piece, :, pl.ds(own_part, 16), :]
            for j in range(4):
                wide = source[side, :, j].astype(F32).reshape(256, 128)
                squares = wide * wide if squares is None else squares + wide * wide
                row = gain[pl.ds(number(*BLOCKS[at + i], j // 2) * 2 + j % 2, 1), :]
                xs[:, i * 512 + j * 128 : i * 512 + (j + 1) * 128] = (wide * row).astype(BF16)
        if copies is not None:
            for i in pair:
                for copy in copies[i]:
                    copy.wait()
        span = slice(start * 512, (pair[-1] + 1) * 512)
        for side in range(2):
            cols = slice(side * 512, (side + 1) * 512)
            if side == 0:
                part = jnp.dot(xs[:, span], lexs[span, :], preferred_element_type=F32)
            else:
                part = 0.0
                for i in pair:
                    for half in range(2):
                        row = pl.multiple_of(number(*BLOCKS[at + i], half) * 256, 256)
                        x_cols = slice(i * 512 + half * 256, i * 512 + (half + 1) * 256)
                        part += jnp.dot(
                            xs[:, x_cols], lex_peer[pl.ds(row, 256), :], preferred_element_type=F32
                        )
            if start:
                z_out[:, cols] += part
            elif first:
                z_out[:, cols] = part
            else:
                z_out[:, cols] = z_in[:, cols] + part
    if not last:
        sq_out[...] = squares
    if following:
        for group in next_copies:
            for copy in group:
                copy.wait()
    if last:
        sharp = column_of(sharp_ref[...], held)
        chosen = column_of(chosen_ref[...].astype(F32), held).astype(jnp.int32)
        scale = lax.rsqrt(jnp.sum(squares, axis=1, keepdims=True) / 8192.0 + 1e-05) * sharp
        z = z_out[...] * scale
        z_out[...] = z
        top = jnp.max(z, axis=1, keepdims=True)
        lse = top + jnp.log(jnp.sum(jnp.exp(z - top), axis=1, keepdims=True))
        token = jnp.zeros((256, 1), F32)
        for side in range(2):
            base = (((x * 2 + (c if side == 0 else 1 - c)) * 8 + t) * 4 + y) * 512
            here = lax.broadcasted_iota(jnp.int32, (256, 512), 1) == chosen - base
            part = jnp.where(here, z[:, side * 512 : (side + 1) * 512], 0.0)
            token += jnp.sum(part, axis=1, keepdims=True)
        odd = lax.broadcasted_iota(jnp.int32, (256, 128), 0) % 2
        low, high = rows_of(lse, 256)
        lse_out[...] = jnp.where(odd == 0, low, high)
        low, high = rows_of(token, 256)
        tok_out[0:1, :] = low
        tok_out[1:2, :] = high


def head_call(sources, at, following, gain, lex_own, lex_peer, state, lexs, closing):
    sides = [source.shape[0] for source in sources]
    total = sum(sides)
    first, ready, last = state is None, lexs is not None, closing is not None
    vmem, anywhere = pl.BlockSpec(), pl.BlockSpec(memory_space=pl.ANY)
    in_specs = [vmem] * (len(sources) + 1) + [anywhere, vmem]
    operands = [*sources, gain, in_hbm(lex_own), in_vmem(lex_peer)]
    for extra in (state, lexs, closing):
        if extra is not None:
            operands += list(extra)
            in_specs += [vmem] * len(extra)
    out_shape = [
        jax.ShapeDtypeStruct((256, 1024), F32),
        jax.ShapeDtypeStruct((total, 4, 16, 128), BF16),
    ]
    scratch = []
    if last:
        out_shape += [
            jax.ShapeDtypeStruct((256, 128), F32),
            jax.ShapeDtypeStruct((2, 128), F32),
        ]
    else:
        out_shape += [jax.ShapeDtypeStruct((256, 128), F32)]
    if following:
        out_shape += [pltpu.VMEM((512 * following, 512), BF16)]
    if first:
        out_shape += [jax.ShapeDtypeStruct(source.shape, source.dtype) for source in sources]
    if not ready:
        scratch += [pltpu.VMEM((512 * total, 512), BF16), pltpu.SemaphoreType.DMA((2 * total,))]
    if following:
        scratch += [pltpu.SemaphoreType.DMA((2 * following,))]
    scratch += [pltpu.VMEM((256, 512 * total), BF16), pltpu.VMEM((128, 128), F32)]
    return pl.pallas_call(
        functools.partial(head_body, (sides, at, ready, following, first, last)),
        in_specs=in_specs,
        out_shape=out_shape,
        scratch_shapes=scratch,
        compiler_params=pltpu.CompilerParams(vmem_limit_bytes=LIMIT),
        cost_estimate=pl.CostEstimate(
            flops=2 * 256 * 512 * 1024 * total,
            bytes_accessed=total * (2**20 + 2**18) + 2**21,
            transcendentals=0,
        ),
    )(*operands)


def pile_body(first_ref, second_ref, out_ref):
    out_ref[0] = first_ref[...]
    out_ref[1] = second_ref[...]


def pile(first, second):
    return pl.pallas_call(
        pile_body,
        out_shape=jax.ShapeDtypeStruct((2, 8, 4, 32, 128), BF16),
        compiler_params=pltpu.CompilerParams(vmem_limit_bytes=LIMIT),
        cost_estimate=pl.CostEstimate(flops=0, bytes_accessed=2**20, transcendentals=0),
    )(first, second)


def mass_body(z_ref, lse_ref, tok_ref, level_ref, *refs):
    picks, (out_ref, norm_out, hidden_out, heap, held) = refs[:-5], refs[-5:]
    at = 0
    for pick in picks:
        heap[at : at + pick.shape[0]] = pick[...]
        at += pick.shape[0]
    x, c, t, y = place()
    spots = [(far % 4, side % 4) for far, side in BLOCKS]
    for yb in range(4):
        dx, dy = (t // 2 - x + 4) % 4, (yb - y + 4) % 4
        far, side = jnp.where(c == 0, dx, dy), jnp.where(c == 0, dy, dx)
        spot = jnp.int32(0)
        for i, (f, s) in enumerate(spots):
            spot = jnp.where((far == f) & (side == s), i, spot)
        piece = heap[spot]
        for j in range(2):
            cols = slice(yb * 256 + j * 128, yb * 256 + (j + 1) * 128)
            hidden_out[:, cols] = jnp.where(t % 2 == c, piece[j], piece[2 + j])
    level = column_of(level_ref[...], held)
    parts = lse_ref[...]
    odd = lax.broadcasted_iota(jnp.int32, parts.shape, 0) % 2
    columns = []
    for h in range(2):
        top = jnp.max(jnp.where(odd == h, parts, -jnp.inf), axis=0, keepdims=True)
        total = jnp.sum(jnp.where(odd == h, jnp.exp(parts - top), 0.0), axis=0, keepdims=True)
        norm = top + jnp.log(total)
        norm_out[h : h + 1, :] = norm
        columns.append(jnp.transpose(jnp.broadcast_to(norm, (128, 128)))[:, :1])
    logp = z_ref[...] - jnp.concatenate(columns, axis=0)
    gate = cut_slope * (level + logp * (1.0 / LN2))
    kept = jnp.sum(jnp.exp(logp) / (1.0 + jnp.exp(-gate)), axis=1, keepdims=True)
    low, high = rows_of(kept, 512)
    which = lax.broadcasted_iota(jnp.int32, (512, 128), 0) % 4
    out_ref[...] = jnp.where(
        which == 0,
        low,
        jnp.where(which == 1, high, jnp.where(which == 2, tok_ref[0:1, :], tok_ref[1:2, :])),
    )


def mass_call(z, lse, tok, level, picks):
    return pl.pallas_call(
        mass_body,
        out_shape=[
            jax.ShapeDtypeStruct((512, 128), F32),
            jax.ShapeDtypeStruct((2, 128), F32),
            jax.ShapeDtypeStruct((16, 1024), BF16),
        ],
        scratch_shapes=[pltpu.VMEM((16, 4, 16, 128), BF16), pltpu.VMEM((128, 128), F32)],
        compiler_params=pltpu.CompilerParams(vmem_limit_bytes=LIMIT),
    )(z, lse, tok, level, *picks)


def swap_halves(rows):
    return jnp.concatenate([rows[:, 64:], rows[:, :64]], axis=1)


def surprise_body(got_ref, norm_ref, level_ref, out_ref):
    sums = jnp.sum(got_ref[...].reshape(64, 8, 128), axis=0)
    sums = sums[:4] + sums[4:]
    kept, token = sums[:2], sums[2:]
    table = level_ref[...]
    turned = swap_halves(table)
    even = lax.axis_index("core") == 0
    first, second = jnp.where(even, table, turned), jnp.where(even, turned, table)
    low = lax.broadcasted_iota(jnp.int32, (1, 128), 1) < 64
    level = jnp.concatenate(
        [jnp.where(low, first[2 * h : 2 * h + 1], second[2 * h + 1 : 2 * h + 2]) for h in range(2)]
    )
    token_logp = token - norm_ref[...]
    gate = cut_slope * (level + token_logp / LN2)
    log_gate = jnp.minimum(gate, 0.0) - jnp.log1p(jnp.exp(-jnp.abs(gate)))
    out_ref[...] = -(token_logp + log_gate - jnp.log(kept)) / LN2


def surprise_call(got, norm, level):
    return pl.pallas_call(
        surprise_body,
        out_shape=jax.ShapeDtypeStruct((2, 128), F32),
        compiler_params=pltpu.CompilerParams(vmem_limit_bytes=LIMIT),
    )(got, norm, level)


def merge_body(own_ref, peer_ref, level_ref, surprise_out, next_out):
    even = lax.axis_index("core") == 0
    own, peer = own_ref[...], peer_ref[...]
    evens, odds = jnp.where(even, own, peer), jnp.where(even, peer, own)
    low = lax.broadcasted_iota(jnp.int32, (1, 128), 1) < 64
    first = jnp.where(low, evens, swap_halves(odds))
    second = jnp.where(low, swap_halves(evens), odds)
    surprise = jnp.concatenate([first[:1], second[:1], first[1:], second[1:]])
    surprise_out[...] = surprise
    next_out[...] = level_ref[...] - 0.1 * (surprise - 5.0)


def merge_call(own, peer, level):
    return pl.pallas_call(
        merge_body,
        out_shape=[jax.ShapeDtypeStruct((4, 128), F32)] * 2,
        compiler_params=pltpu.CompilerParams(vmem_limit_bytes=LIMIT),
    )(own, peer, level)


def shards(
    probe_vectors,
    stored_lookup_vectors,
    stored_content_vectors,
    fresh_lookup_vector,
    fresh_content_vector,
    history_counts,
    mixing_matrix,
    skip_stream,
    closing_multiplier,
    lexicon_matrix,
    sharpening_factor,
    desired_perplexity,
    chosen_symbols,
):
    mix_peer = swap_core(mixing_matrix)

    sent, mix_own = attend(
        probe_vectors,
        stored_lookup_vectors,
        stored_content_vectors,
        fresh_lookup_vector,
        fresh_content_vector,
        history_counts,
        skip_stream,
        mixing_matrix,
    )
    lexicon_matrix, mix_peer, sent = lax.optimization_barrier((lexicon_matrix, mix_peer, sent))
    lex_peer = swap_core(lexicon_matrix)
    got = lax.all_to_all(sent, ("x", "rep"), 0, 0, tiled=True).reshape(256, 1280)
    gain_rows = closing_multiplier.reshape(8, 128)
    sent = project(got, mix_own, mix_peer, gain_rows)
    got = lax.all_to_all(sent, "tensor", 0, 0, tiled=True)
    sent, gain = total_call(got)

    own = lax.all_to_all(sent, "tensor", 0, 0, tiled=True).reshape(8, 4, 32, 128)
    side = lambda v, s: lax.ppermute(v, PLANE, turn_other(s))
    far = lambda v, s: lax.ppermute(v, PLANE, turn(s))
    ahead, behind, across = side(own, 1), side(own, -1), side(own, 2)
    low = pile(own, behind)
    ahead, across, low = lax.optimization_barrier((ahead, across, low))
    high = pile(ahead, across)
    left_low, right_high = far(low, 1), far(high, -1)
    past_low, past_high = far(left_low, 1), far(right_high, -1)

    fixed = (gain, lexicon_matrix, lex_peer)
    z, pick_0, sq, low, high = head_call([low, high], 0, 0, *fixed, None, None, None)
    left_high, right_low = far(high, 1), far(low, -1)
    z, pick_1, sq = head_call([left_low, right_high], 4, 0, *fixed, (z, sq), None, None)
    z, pick_2, sq, lexs = head_call([left_high, right_low], 8, 4, *fixed, (z, sq), None, None)
    closing = (sharpening_factor.reshape(4, 128), chosen_symbols.reshape(4, 128))
    z, pick_3, lse, tok = head_call(
        [past_low, past_high], 12, 0, *fixed, (z, sq), (lexs,), closing
    )
    picked = [pick_0, pick_1, pick_2, pick_3]
    every_lse = lax.all_to_all(lse.reshape(128, 2, 128), SAME_CORE, 0, 0, tiled=True)
    levels = desired_perplexity.reshape(4, 128)
    sent, norm, hidden = mass_call(z, every_lse.reshape(256, 128), tok, levels, picked)
    got = lax.all_to_all(sent.reshape(128, 4, 128), SAME_CORE, 0, 0, tiled=True)
    mine = surprise_call(got.reshape(512, 128), norm, levels)
    surprise, next_targets = merge_call(mine, swap_core(mine), levels)
    surprise, next_targets = surprise.reshape(512), next_targets.reshape(512)
    return (hidden, next_targets, surprise)


def solution(mesh):
    fine = Mesh(mesh.devices.reshape(4, 2, 8, 4), ("x", "core", "tensor", "rep"))
    rows = ("x", "core", "rep")
    placed = (
        P(rows, "tensor", None),
        P(rows, "tensor", None, None),
        P(rows, "tensor", None, None),
        P(rows, "tensor", None),
        P(rows, "tensor", None),
        P(rows),
        P("tensor", rows),
        P(rows, "tensor"),
        P("tensor"),
        P(None, ("x", "core", "tensor", "rep")),
        P(),
        P(),
        P(),
    )
    return jax.shard_map(
        shards,
        mesh=fine,
        in_specs=placed,
        out_specs=(P(rows, "tensor"), P(), P()),
        check_vma=False,
    )
```

```python
import functools
import math

import jax
import jax.numpy as jnp
from jax import lax
from jax.experimental import pallas as pl
from jax.experimental.pallas import tpu as pltpu
from jax.sharding import Mesh
from jax.sharding import PartitionSpec as P

cut_slope = 4.0
LN2 = math.log(2.0)
F32 = jnp.float32
BF16 = jnp.bfloat16
PLANE = ("x", "core", "rep")
EVERY = ("x", "core", "tensor", "rep")
SAME_CORE = ("x", "tensor", "rep")
LIMIT = 16 * 1024 * 1024


def place():
    return tuple(lax.axis_index(name) for name in ("x", "core", "tensor", "rep"))


def number(far, side, half):
    x, c, _, y = place()
    even = c == 0
    bx = jnp.where(even, x + (far % 4), x + (side % 4)) % 4
    by = jnp.where(even, y + (side % 4), y + (far % 4)) % 4
    return (bx * 2 + (c if half == 0 else 1 - c)) * 4 + by


def column_of(table, held):
    c = lax.axis_index("core")
    held[...] = jnp.transpose(jnp.concatenate([table, jnp.zeros((124, 128), F32)]))
    start = pl.multiple_of(c * 64, 64)
    return jnp.concatenate([held[pl.ds(start, 64), i : i + 1] for i in range(4)])


LOWS, HIGHS = (0, 1), (-1, 2)
BLOCKS = [
    (far, side)
    for far, sides in (
        (0, LOWS),
        (0, HIGHS),
        (-1, LOWS),
        (1, HIGHS),
        (-1, HIGHS),
        (1, LOWS),
        (2, LOWS),
        (2, HIGHS),
    )
    for side in sides
]


def in_hbm(value):
    return pltpu.with_memory_space_constraint(value, pltpu.HBM)


def in_vmem(value):
    return pltpu.with_memory_space_constraint(value, pltpu.VMEM)


def attend_body(
    counts, q_ref, k_hbm, v_hbm, own_k_ref, own_v_ref, skip_ref, mix, out_ref, mix_out, *scratch
):
    k_ref, v_ref, own_k, own_v, held, sems, mix_sem = scratch
    rows = 8
    groups = k_ref.shape[0] // rows
    score_scale = 1.0 / math.sqrt(k_ref.shape[3])
    copies = []
    for group in range(groups):
        span = pl.ds(group * rows, rows)
        pair = [
            pltpu.make_async_copy(k_hbm.at[span], k_ref.at[span], sems.at[2 * group]),
            pltpu.make_async_copy(v_hbm.at[span], v_ref.at[span], sems.at[2 * group + 1]),
        ]
        for copy in pair:
            copy.start()
        copies.append(pair)
    mix_copy = pltpu.make_async_copy(mix, mix_out, mix_sem)
    mix_copy.start()
    own_k[...] = own_k_ref[...].astype(F32)
    own_v[...] = own_v_ref[...].astype(F32)
    for there in range(16):
        block = there % 4
        out_ref[there, :, 1024:] = skip_ref[:, block * 256 : (block + 1) * 256]

    for group in range(groups):
        first = group * rows
        spread = lambda ref: jnp.concatenate(
            [jnp.broadcast_to(ref[first + row : first + row + 1], (8, 128)) for row in range(rows)]
        )
        q = q_ref[first : first + rows].reshape(rows * 8, 128)
        own = score_scale * jnp.sum(q.astype(F32) * spread(own_k), axis=1, keepdims=True)
        copies[group][0].wait()
        scores = score_scale * jnp.concatenate(
            [
                lax.dot_general(
                    q_ref[first + row],
                    k_ref[first + row, 0],
                    (((1,), (1,)), ((), ())),
                    preferred_element_type=F32,
                )
                for row in range(rows)
            ]
        )
        position = lax.broadcasted_iota(jnp.int32, (8, scores.shape[1]), 1)
        live = jnp.concatenate([position < counts[first + row] for row in range(rows)])
        top = jnp.maximum(jnp.max(jnp.where(live, scores, -1e30), axis=1, keepdims=True), own)
        expo = jnp.where(live, jnp.exp(scores - top), 0.0)
        own_expo = jnp.exp(own - top)
        total = jnp.sum(expo, axis=1, keepdims=True) + own_expo
        weights = expo.astype(BF16)
        copies[group][1].wait()
        accum = jnp.concatenate(
            [
                jnp.dot(
                    weights[row * 8 : (row + 1) * 8],
                    v_ref[first + row, 0],
                    preferred_element_type=F32,
                )
                for row in range(rows)
            ]
        )
        accum = accum + own_expo.astype(BF16).astype(F32) * spread(own_v)
        held[first * 8 : (first + rows) * 8, :] = accum / total

    for h in range(8):
        piece = held[pl.ds(h, 16, stride=8), :].astype(BF16)
        for there in range(16):
            out_ref[there, :, h * 128 : (h + 1) * 128] = piece
    mix_copy.wait()


def attend(q, k, v, own_k, own_v, counts, skip, mix):
    vmem, anywhere = pl.BlockSpec(), pl.BlockSpec(memory_space=pl.ANY)
    own_k, own_v = own_k.reshape(16, 128), own_v.reshape(16, 128)
    return pl.pallas_call(
        attend_body,
        in_specs=[
            pl.BlockSpec(memory_space=pltpu.SMEM),
            vmem,
            anywhere,
            anywhere,
            vmem,
            vmem,
            vmem,
            anywhere,
        ],
        out_shape=[
            jax.ShapeDtypeStruct((16, 16, 1280), BF16),
            pltpu.VMEM((1024, 256), BF16),
        ],
        scratch_shapes=[
            pltpu.VMEM((16, 1, 512, 128), BF16),
            pltpu.VMEM((16, 1, 512, 128), BF16),
            pltpu.VMEM((16, 128), F32),
            pltpu.VMEM((16, 128), F32),
            pltpu.VMEM((128, 128), F32),
            pltpu.SemaphoreType.DMA((8,)),
            pltpu.SemaphoreType.DMA,
        ],
        compiler_params=pltpu.CompilerParams(vmem_limit_bytes=LIMIT),
    )(*[in_hbm(value) for value in (counts, q, k, v, own_k, own_v, skip, mix)])


def project_body(got_ref, own_ref, peer_ref, gain_ref, out_ref):
    attn = got_ref[:, :1024]
    skip = got_ref[:, 1024:].astype(F32)
    x, c, t, _ = place()
    for side, mix_ref in enumerate((own_ref, peer_ref)):
        part = jnp.dot(attn, mix_ref[...], preferred_element_type=F32)
        holds = t == 2 * x + (c if side == 0 else 1 - c)
        part = jnp.where(holds, part + skip, part).astype(BF16)
        for j in range(2):
            cols = part[:, j * 128 : (j + 1) * 128].reshape(8, 32, 128)
            out_ref[:, (2 * side + j) * 32 : (2 * side + j + 1) * 32, :] = cols
    gain = gain_ref[...]
    for there in range(8):
        out_ref[there, 128:, :] = gain


def project(got, mix_own, mix_peer, gain):
    return pl.pallas_call(
        project_body,
        out_shape=jax.ShapeDtypeStruct((8, 136, 128), BF16),
        compiler_params=pltpu.CompilerParams(vmem_limit_bytes=LIMIT),
    )(got, mix_own, mix_peer, gain)


def total_body(got_ref, out_ref, gain_ref):
    total = got_ref[0, :128, :].astype(F32)
    for source in range(1, 8):
        total += got_ref[source, :128, :].astype(F32)
    total = total.astype(BF16)
    for there in range(8):
        out_ref[there] = total
    for there in range(8):
        gain_ref[there * 8 : (there + 1) * 8, :] = got_ref[there, 128:, :].astype(F32)


def total_call(got):
    return pl.pallas_call(
        total_body,
        out_shape=[
            jax.ShapeDtypeStruct((8, 128, 128), BF16),
            jax.ShapeDtypeStruct((64, 128), F32),
        ],
        compiler_params=pltpu.CompilerParams(vmem_limit_bytes=LIMIT),
    )(got)


def turn(shift):
    pairs = []
    for x in range(4):
        for c in range(2):
            for y in range(4):
                here = (x * 2 + c) * 4 + y
                if c == 0:
                    there = (((x + shift) % 4) * 2 + c) * 4 + y
                else:
                    there = (x * 2 + c) * 4 + (y + shift) % 4
                pairs.append((here, there))
    return pairs


def turn_other(shift):
    pairs = []
    for x in range(4):
        for c in range(2):
            for y in range(4):
                here = (x * 2 + c) * 4 + y
                if c == 1:
                    there = (((x + shift) % 4) * 2 + c) * 4 + y
                else:
                    there = (x * 2 + c) * 4 + (y + shift) % 4
                pairs.append((here, there))
    return pairs


def swap_core(value):
    return lax.ppermute(value, "core", [(0, 1), (1, 0)])


def rows_of(column, copies):
    wide = jnp.broadcast_to(column, (256, 128))
    return [jnp.transpose(wide[h * 128 : (h + 1) * 128])[:1] for h in range(2)]


def fetch(lexicon, at, count, target, sems):
    copies = []
    for i in range(count):
        group = []
        for half in range(2):
            row = pl.multiple_of(number(*BLOCKS[at + i], half) * 256, 256)
            copy = pltpu.make_async_copy(
                lexicon.at[pl.ds(row, 256), :],
                target.at[pl.ds(i * 512 + half * 256, 256), :],
                sems.at[2 * i + half],
            )
            copy.start()
            group.append(copy)
        copies.append(group)
    return copies


def head_body(plan, *refs):
    sides, at, ready, following, first, last = plan
    refs = list(refs)
    take = lambda n: [refs.pop(0) for _ in range(n)]
    total = sum(sides)
    sources = take(len(sides))
    gain, lex_own, lex_peer = take(3)
    if not first:
        z_in, sq_in = take(2)
    if ready:
        (lexs,) = take(1)
    if last or following:
        sharp_ref, chosen_ref = take(2)
    if last:
        z_out, pick_out, lse_out, tok_out = take(4)
    else:
        z_out, pick_out, sq_out = take(3)
    if following:
        lex_next, sharp_out, chosen_out = take(3)
    if first:
        for source, copy_out in zip(sources, take(len(sources))):
            copy_out[...] = source[...]
    copies = None
    if not ready:
        lexs, sems = take(2)
        copies = fetch(lex_own, at, total, lexs, sems)
    if following:
        next_copies = fetch(lex_own, at + total, following, lex_next, *take(1))
    xs, held = take(2)
    x, c, t, y = place()
    mine = x * 4 + y
    squares = None if first else sq_in[...]
    own_piece, own_part = mine // 2, pl.multiple_of((mine % 2) * 16, 16)
    places = [(source, side) for source, some in zip(sources, sides) for side in range(some)]
    for start in range(0, total, 2):
        pair = range(start, min(start + 2, total))
        for i in pair:
            source, side = places[i]
            pick_out[i] = source[side, own_piece, :, pl.ds(own_part, 16), :]
            for j in range(4):
                wide = source[side, :, j].astype(F32).reshape(256, 128)
                squares = wide * wide if squares is None else squares + wide * wide
                row = gain[pl.ds(number(*BLOCKS[at + i], j // 2) * 2 + j % 2, 1), :]
                xs[:, i * 512 + j * 128 : i * 512 + (j + 1) * 128] = (wide * row).astype(BF16)
        if copies is not None:
            for i in pair:
                for copy in copies[i]:
                    copy.wait()
        span = slice(start * 512, (pair[-1] + 1) * 512)
        for side in range(2):
            cols = slice(side * 512, (side + 1) * 512)
            if side == 0:
                part = jnp.dot(xs[:, span], lexs[span, :], preferred_element_type=F32)
            else:
                part = 0.0
                for i in pair:
                    for half in range(2):
                        row = pl.multiple_of(number(*BLOCKS[at + i], half) * 256, 256)
                        x_cols = slice(i * 512 + half * 256, i * 512 + (half + 1) * 256)
                        part += jnp.dot(
                            xs[:, x_cols], lex_peer[pl.ds(row, 256), :], preferred_element_type=F32
                        )
            if start:
                z_out[:, cols] += part
            elif first:
                z_out[:, cols] = part
            else:
                z_out[:, cols] = z_in[:, cols] + part
    if not last:
        sq_out[...] = squares
    if following:
        sharp_out[...] = column_of(sharp_ref[...], held)
        chosen_out[...] = column_of(chosen_ref[...].astype(F32), held)
        for group in next_copies:
            for copy in group:
                copy.wait()
    if last:
        sharp = sharp_ref[...]
        chosen = chosen_ref[...].astype(jnp.int32)
        scale = lax.rsqrt(jnp.sum(squares, axis=1, keepdims=True) / 8192.0 + 1e-05) * sharp
        z = z_out[...] * scale
        z_out[...] = z
        top = jnp.max(z, axis=1, keepdims=True)
        lse = top + jnp.log(jnp.sum(jnp.exp(z - top), axis=1, keepdims=True))
        token = jnp.zeros((256, 1), F32)
        for side in range(2):
            base = (((x * 2 + (c if side == 0 else 1 - c)) * 8 + t) * 4 + y) * 512
            here = lax.broadcasted_iota(jnp.int32, (256, 512), 1) == chosen - base
            part = jnp.where(here, z[:, side * 512 : (side + 1) * 512], 0.0)
            token += jnp.sum(part, axis=1, keepdims=True)
        odd = lax.broadcasted_iota(jnp.int32, (256, 128), 0) % 2
        low, high = rows_of(lse, 256)
        lse_out[...] = jnp.where(odd == 0, low, high)
        low, high = rows_of(token, 256)
        tok_out[0:1, :] = low
        tok_out[1:2, :] = high


def head_call(sources, at, following, gain, lex_own, lex_peer, state, lexs, closing):
    sides = [source.shape[0] for source in sources]
    total = sum(sides)
    first, ready, last = state is None, lexs is not None, closing is not None and not following
    vmem, anywhere = pl.BlockSpec(), pl.BlockSpec(memory_space=pl.ANY)
    in_specs = [vmem] * (len(sources) + 1) + [anywhere, vmem]
    operands = [*sources, gain, in_hbm(lex_own), in_vmem(lex_peer)]
    for extra in (state, lexs, closing):
        if extra is not None:
            operands += list(extra)
            in_specs += [vmem] * len(extra)
    out_shape = [
        jax.ShapeDtypeStruct((256, 1024), F32),
        jax.ShapeDtypeStruct((total, 4, 16, 128), BF16),
    ]
    scratch = []
    if last:
        out_shape += [
            jax.ShapeDtypeStruct((256, 128), F32),
            jax.ShapeDtypeStruct((2, 128), F32),
        ]
    else:
        out_shape += [jax.ShapeDtypeStruct((256, 128), F32)]
    if following:
        out_shape += [pltpu.VMEM((512 * following, 512), BF16)]
        out_shape += [pltpu.VMEM((256, 1), F32)] * 2
    if first:
        out_shape += [jax.ShapeDtypeStruct(source.shape, source.dtype) for source in sources]
    if not ready:
        scratch += [pltpu.VMEM((512 * total, 512), BF16), pltpu.SemaphoreType.DMA((2 * total,))]
    if following:
        scratch += [pltpu.SemaphoreType.DMA((2 * following,))]
    scratch += [pltpu.VMEM((256, 512 * total), BF16), pltpu.VMEM((128, 128), F32)]
    return pl.pallas_call(
        functools.partial(head_body, (sides, at, ready, following, first, last)),
        in_specs=in_specs,
        out_shape=out_shape,
        scratch_shapes=scratch,
        compiler_params=pltpu.CompilerParams(vmem_limit_bytes=LIMIT),
        cost_estimate=pl.CostEstimate(
            flops=2 * 256 * 512 * 1024 * total,
            bytes_accessed=total * (2**20 + 2**18) + 2**21,
            transcendentals=0,
        ),
    )(*operands)


def pile_body(first_ref, second_ref, out_ref):
    out_ref[0] = first_ref[...]
    out_ref[1] = second_ref[...]


def pile(first, second):
    return pl.pallas_call(
        pile_body,
        out_shape=jax.ShapeDtypeStruct((2, 8, 4, 32, 128), BF16),
        compiler_params=pltpu.CompilerParams(vmem_limit_bytes=LIMIT),
        cost_estimate=pl.CostEstimate(flops=0, bytes_accessed=2**20, transcendentals=0),
    )(first, second)


def mass_body(z_ref, lse_ref, tok_ref, level_ref, *refs):
    picks, (out_ref, norm_out, hidden_out, heap, held) = refs[:-5], refs[-5:]
    at = 0
    for pick in picks:
        heap[at : at + pick.shape[0]] = pick[...]
        at += pick.shape[0]
    x, c, t, y = place()
    spots = [(far % 4, side % 4) for far, side in BLOCKS]
    for yb in range(4):
        dx, dy = (t // 2 - x + 4) % 4, (yb - y + 4) % 4
        far, side = jnp.where(c == 0, dx, dy), jnp.where(c == 0, dy, dx)
        spot = jnp.int32(0)
        for i, (f, s) in enumerate(spots):
            spot = jnp.where((far == f) & (side == s), i, spot)
        piece = heap[spot]
        for j in range(2):
            cols = slice(yb * 256 + j * 128, yb * 256 + (j + 1) * 128)
            hidden_out[:, cols] = jnp.where(t % 2 == c, piece[j], piece[2 + j])
    level = column_of(level_ref[...], held)
    parts = lse_ref[...]
    odd = lax.broadcasted_iota(jnp.int32, parts.shape, 0) % 2
    columns = []
    for h in range(2):
        top = jnp.max(jnp.where(odd == h, parts, -jnp.inf), axis=0, keepdims=True)
        total = jnp.sum(jnp.where(odd == h, jnp.exp(parts - top), 0.0), axis=0, keepdims=True)
        norm = top + jnp.log(total)
        norm_out[h : h + 1, :] = norm
        columns.append(jnp.transpose(jnp.broadcast_to(norm, (128, 128)))[:, :1])
    logp = z_ref[...] - jnp.concatenate(columns, axis=0)
    gate = cut_slope * (level + logp * (1.0 / LN2))
    kept = jnp.sum(jnp.exp(logp) / (1.0 + jnp.exp(-gate)), axis=1, keepdims=True)
    low, high = rows_of(kept, 512)
    which = lax.broadcasted_iota(jnp.int32, (512, 128), 0) % 4
    out_ref[...] = jnp.where(
        which == 0,
        low,
        jnp.where(which == 1, high, jnp.where(which == 2, tok_ref[0:1, :], tok_ref[1:2, :])),
    )


def mass_call(z, lse, tok, level, picks):
    return pl.pallas_call(
        mass_body,
        out_shape=[
            jax.ShapeDtypeStruct((512, 128), F32),
            jax.ShapeDtypeStruct((2, 128), F32),
            jax.ShapeDtypeStruct((16, 1024), BF16),
        ],
        scratch_shapes=[pltpu.VMEM((16, 4, 16, 128), BF16), pltpu.VMEM((128, 128), F32)],
        compiler_params=pltpu.CompilerParams(vmem_limit_bytes=LIMIT),
    )(z, lse, tok, level, *picks)


def swap_halves(rows):
    return jnp.concatenate([rows[:, 64:], rows[:, :64]], axis=1)


def surprise_body(got_ref, norm_ref, level_ref, out_ref):
    sums = jnp.sum(got_ref[...].reshape(64, 8, 128), axis=0)
    sums = sums[:4] + sums[4:]
    kept, token = sums[:2], sums[2:]
    table = level_ref[...]
    turned = swap_halves(table)
    even = lax.axis_index("core") == 0
    first, second = jnp.where(even, table, turned), jnp.where(even, turned, table)
    low = lax.broadcasted_iota(jnp.int32, (1, 128), 1) < 64
    level = jnp.concatenate(
        [jnp.where(low, first[2 * h : 2 * h + 1], second[2 * h + 1 : 2 * h + 2]) for h in range(2)]
    )
    token_logp = token - norm_ref[...]
    gate = cut_slope * (level + token_logp / LN2)
    log_gate = jnp.minimum(gate, 0.0) - jnp.log1p(jnp.exp(-jnp.abs(gate)))
    out_ref[...] = -(token_logp + log_gate - jnp.log(kept)) / LN2


def surprise_call(got, norm, level):
    return pl.pallas_call(
        surprise_body,
        out_shape=jax.ShapeDtypeStruct((2, 128), F32),
        compiler_params=pltpu.CompilerParams(vmem_limit_bytes=LIMIT),
    )(got, norm, level)


def merge_body(own_ref, peer_ref, level_ref, surprise_out, next_out):
    even = lax.axis_index("core") == 0
    own, peer = own_ref[...], peer_ref[...]
    evens, odds = jnp.where(even, own, peer), jnp.where(even, peer, own)
    low = lax.broadcasted_iota(jnp.int32, (1, 128), 1) < 64
    first = jnp.where(low, evens, swap_halves(odds))
    second = jnp.where(low, swap_halves(evens), odds)
    surprise = jnp.concatenate([first[:1], second[:1], first[1:], second[1:]])
    surprise_out[...] = surprise
    next_out[...] = level_ref[...] - 0.1 * (surprise - 5.0)


def merge_call(own, peer, level):
    return pl.pallas_call(
        merge_body,
        out_shape=[jax.ShapeDtypeStruct((4, 128), F32)] * 2,
        compiler_params=pltpu.CompilerParams(vmem_limit_bytes=LIMIT),
    )(own, peer, level)


def shards(
    probe_vectors,
    stored_lookup_vectors,
    stored_content_vectors,
    fresh_lookup_vector,
    fresh_content_vector,
    history_counts,
    mixing_matrix,
    skip_stream,
    closing_multiplier,
    lexicon_matrix,
    sharpening_factor,
    desired_perplexity,
    chosen_symbols,
):
    mix_peer = swap_core(mixing_matrix)

    sent, mix_own = attend(
        probe_vectors,
        stored_lookup_vectors,
        stored_content_vectors,
        fresh_lookup_vector,
        fresh_content_vector,
        history_counts,
        skip_stream,
        mixing_matrix,
    )
    lexicon_matrix, mix_peer, sent = lax.optimization_barrier((lexicon_matrix, mix_peer, sent))
    lex_peer = swap_core(lexicon_matrix)
    got = lax.all_to_all(sent, ("x", "rep"), 0, 0, tiled=True).reshape(256, 1280)
    gain_rows = closing_multiplier.reshape(8, 128)
    sent = project(got, mix_own, mix_peer, gain_rows)
    got = lax.all_to_all(sent, "tensor", 0, 0, tiled=True)
    sent, gain = total_call(got)

    own = lax.all_to_all(sent, "tensor", 0, 0, tiled=True).reshape(8, 4, 32, 128)
    side = lambda v, s: lax.ppermute(v, PLANE, turn_other(s))
    far = lambda v, s: lax.ppermute(v, PLANE, turn(s))
    ahead, behind, across = side(own, 1), side(own, -1), side(own, 2)
    low = pile(own, behind)
    ahead, across, low = lax.optimization_barrier((ahead, across, low))
    high = pile(ahead, across)
    left_low, right_high = far(low, 1), far(high, -1)
    past_low, past_high = far(left_low, 1), far(right_high, -1)

    fixed = (gain, lexicon_matrix, lex_peer)
    z, pick_0, sq, low, high = head_call([low, high], 0, 0, *fixed, None, None, None)
    left_high, right_low = far(high, 1), far(low, -1)
    z, pick_1, sq = head_call([left_low, right_high], 4, 0, *fixed, (z, sq), None, None)
    closing = (sharpening_factor.reshape(4, 128), chosen_symbols.reshape(4, 128))
    z, pick_2, sq, lexs, *closing = head_call(
        [left_high, right_low], 8, 4, *fixed, (z, sq), None, closing
    )
    z, pick_3, lse, tok = head_call(
        [past_low, past_high], 12, 0, *fixed, (z, sq), (lexs,), closing
    )
    picked = [pick_0, pick_1, pick_2, pick_3]
    every_lse = lax.all_to_all(lse.reshape(128, 2, 128), SAME_CORE, 0, 0, tiled=True)
    levels = desired_perplexity.reshape(4, 128)
    sent, norm, hidden = mass_call(z, every_lse.reshape(256, 128), tok, levels, picked)
    got = lax.all_to_all(sent.reshape(128, 4, 128), SAME_CORE, 0, 0, tiled=True)
    mine = surprise_call(got.reshape(512, 128), norm, levels)
    surprise, next_targets = merge_call(mine, swap_core(mine), levels)
    surprise, next_targets = surprise.reshape(512), next_targets.reshape(512)
    return (hidden, next_targets, surprise)


def solution(mesh):
    fine = Mesh(mesh.devices.reshape(4, 2, 8, 4), ("x", "core", "tensor", "rep"))
    rows = ("x", "core", "rep")
    placed = (
        P(rows, "tensor", None),
        P(rows, "tensor", None, None),
        P(rows, "tensor", None, None),
        P(rows, "tensor", None),
        P(rows, "tensor", None),
        P(rows),
        P("tensor", rows),
        P(rows, "tensor"),
        P("tensor"),
        P(None, ("x", "core", "tensor", "rep")),
        P(),
        P(),
        P(),
    )
    return jax.shard_map(
        shards,
        mesh=fine,
        in_specs=placed,
        out_specs=(P(rows, "tensor"), P(), P()),
        check_vma=False,
    )
```

```python
import functools
import math

import jax
import jax.numpy as jnp
from jax import lax
from jax.experimental import pallas as pl
from jax.experimental.pallas import tpu as pltpu
from jax.sharding import Mesh
from jax.sharding import PartitionSpec as P

cut_slope = 4.0
LN2 = math.log(2.0)
F32 = jnp.float32
BF16 = jnp.bfloat16
PLANE = ("x", "core", "rep")
EVERY = ("x", "core", "tensor", "rep")
SAME_CORE = ("x", "tensor", "rep")
LIMIT = 16 * 1024 * 1024


def place():
    return tuple(lax.axis_index(name) for name in ("x", "core", "tensor", "rep"))


def number(far, side, half):
    x, c, _, y = place()
    even = c == 0
    bx = jnp.where(even, x + (far % 4), x + (side % 4)) % 4
    by = jnp.where(even, y + (side % 4), y + (far % 4)) % 4
    return (bx * 2 + (c if half == 0 else 1 - c)) * 4 + by


def column_of(table, held):
    c = lax.axis_index("core")
    held[...] = jnp.transpose(jnp.concatenate([table, jnp.zeros((124, 128), F32)]))
    start = pl.multiple_of(c * 64, 64)
    return jnp.concatenate([held[pl.ds(start, 64), i : i + 1] for i in range(4)])


LOWS, HIGHS = (0, 1), (-1, 2)
BLOCKS = [
    (far, side)
    for far, sides in (
        (0, LOWS),
        (0, HIGHS),
        (-1, LOWS),
        (1, HIGHS),
        (-1, HIGHS),
        (1, LOWS),
        (2, LOWS),
        (2, HIGHS),
    )
    for side in sides
]


def in_hbm(value):
    return pltpu.with_memory_space_constraint(value, pltpu.HBM)


def in_vmem(value):
    return pltpu.with_memory_space_constraint(value, pltpu.VMEM)


def attend_body(
    counts, q_ref, k_hbm, v_hbm, own_k_ref, own_v_ref, skip_ref, mix, out_ref, mix_out, *scratch
):
    k_ref, v_ref, own_k, own_v, held, sems, mix_sem = scratch
    rows = 8
    groups = k_ref.shape[0] // rows
    score_scale = 1.0 / math.sqrt(k_ref.shape[3])
    copies = []
    for group in range(groups):
        span = pl.ds(group * rows, rows)
        pair = [
            pltpu.make_async_copy(k_hbm.at[span], k_ref.at[span], sems.at[2 * group]),
            pltpu.make_async_copy(v_hbm.at[span], v_ref.at[span], sems.at[2 * group + 1]),
        ]
        for copy in pair:
            copy.start()
        copies.append(pair)
    mix_copy = pltpu.make_async_copy(mix, mix_out, mix_sem)
    mix_copy.start()
    own_k[...] = own_k_ref[...].astype(F32)
    own_v[...] = own_v_ref[...].astype(F32)
    for there in range(16):
        block = there % 4
        out_ref[there, :, 1024:] = skip_ref[:, block * 256 : (block + 1) * 256]

    for group in range(groups):
        first = group * rows
        spread = lambda ref: jnp.concatenate(
            [jnp.broadcast_to(ref[first + row : first + row + 1], (8, 128)) for row in range(rows)]
        )
        q = q_ref[first : first + rows].reshape(rows * 8, 128)
        own = score_scale * jnp.sum(q.astype(F32) * spread(own_k), axis=1, keepdims=True)
        copies[group][0].wait()
        scores = score_scale * jnp.concatenate(
            [
                lax.dot_general(
                    q_ref[first + row],
                    k_ref[first + row, 0],
                    (((1,), (1,)), ((), ())),
                    preferred_element_type=F32,
                )
                for row in range(rows)
            ]
        )
        position = lax.broadcasted_iota(jnp.int32, (8, scores.shape[1]), 1)
        live = jnp.concatenate([position < counts[first + row] for row in range(rows)])
        top = jnp.maximum(jnp.max(jnp.where(live, scores, -1e30), axis=1, keepdims=True), own)
        expo = jnp.where(live, jnp.exp(scores - top), 0.0)
        own_expo = jnp.exp(own - top)
        total = jnp.sum(expo, axis=1, keepdims=True) + own_expo
        weights = expo.astype(BF16)
        copies[group][1].wait()
        accum = jnp.concatenate(
            [
                jnp.dot(
                    weights[row * 8 : (row + 1) * 8],
                    v_ref[first + row, 0],
                    preferred_element_type=F32,
                )
                for row in range(rows)
            ]
        )
        accum = accum + own_expo.astype(BF16).astype(F32) * spread(own_v)
        held[first * 8 : (first + rows) * 8, :] = accum / total

    for h in range(8):
        piece = held[pl.ds(h, 16, stride=8), :].astype(BF16)
        for there in range(16):
            out_ref[there, :, h * 128 : (h + 1) * 128] = piece
    mix_copy.wait()


def attend(q, k, v, own_k, own_v, counts, skip, mix):
    vmem, anywhere = pl.BlockSpec(), pl.BlockSpec(memory_space=pl.ANY)
    own_k, own_v = own_k.reshape(16, 128), own_v.reshape(16, 128)
    return pl.pallas_call(
        attend_body,
        in_specs=[
            pl.BlockSpec(memory_space=pltpu.SMEM),
            vmem,
            anywhere,
            anywhere,
            vmem,
            vmem,
            vmem,
            anywhere,
        ],
        out_shape=[
            jax.ShapeDtypeStruct((16, 16, 1280), BF16),
            pltpu.VMEM((1024, 256), BF16),
        ],
        scratch_shapes=[
            pltpu.VMEM((16, 1, 512, 128), BF16),
            pltpu.VMEM((16, 1, 512, 128), BF16),
            pltpu.VMEM((16, 128), F32),
            pltpu.VMEM((16, 128), F32),
            pltpu.VMEM((128, 128), F32),
            pltpu.SemaphoreType.DMA((8,)),
            pltpu.SemaphoreType.DMA,
        ],
        compiler_params=pltpu.CompilerParams(vmem_limit_bytes=LIMIT),
    )(*[in_hbm(value) for value in (counts, q, k, v, own_k, own_v, skip, mix)])


def project_body(got_ref, own_ref, peer_ref, gain_ref, out_ref):
    attn = got_ref[:, :1024]
    skip = got_ref[:, 1024:].astype(F32)
    x, c, t, _ = place()
    for side, mix_ref in enumerate((own_ref, peer_ref)):
        part = jnp.dot(attn, mix_ref[...], preferred_element_type=F32)
        holds = t == 2 * x + (c if side == 0 else 1 - c)
        part = jnp.where(holds, part + skip, part).astype(BF16)
        for j in range(2):
            cols = part[:, j * 128 : (j + 1) * 128].reshape(8, 32, 128)
            out_ref[:, (2 * side + j) * 32 : (2 * side + j + 1) * 32, :] = cols
    gain = gain_ref[...]
    for there in range(8):
        out_ref[there, 128:, :] = gain


def project(got, mix_own, mix_peer, gain):
    return pl.pallas_call(
        project_body,
        out_shape=jax.ShapeDtypeStruct((8, 136, 128), BF16),
        compiler_params=pltpu.CompilerParams(vmem_limit_bytes=LIMIT),
    )(got, mix_own, mix_peer, gain)


def total_body(got_ref, out_ref, gain_ref):
    total = got_ref[0, :128, :].astype(F32)
    for source in range(1, 8):
        total += got_ref[source, :128, :].astype(F32)
    total = total.astype(BF16)
    for there in range(8):
        out_ref[there] = total
    for there in range(8):
        gain_ref[there * 8 : (there + 1) * 8, :] = got_ref[there, 128:, :].astype(F32)


def total_call(got):
    return pl.pallas_call(
        total_body,
        out_shape=[
            jax.ShapeDtypeStruct((8, 128, 128), BF16),
            jax.ShapeDtypeStruct((64, 128), F32),
        ],
        compiler_params=pltpu.CompilerParams(vmem_limit_bytes=LIMIT),
    )(got)


def turn(shift):
    pairs = []
    for x in range(4):
        for c in range(2):
            for y in range(4):
                here = (x * 2 + c) * 4 + y
                if c == 0:
                    there = (((x + shift) % 4) * 2 + c) * 4 + y
                else:
                    there = (x * 2 + c) * 4 + (y + shift) % 4
                pairs.append((here, there))
    return pairs


def turn_other(shift):
    pairs = []
    for x in range(4):
        for c in range(2):
            for y in range(4):
                here = (x * 2 + c) * 4 + y
                if c == 1:
                    there = (((x + shift) % 4) * 2 + c) * 4 + y
                else:
                    there = (x * 2 + c) * 4 + (y + shift) % 4
                pairs.append((here, there))
    return pairs


def swap_core(value):
    return lax.ppermute(value, "core", [(0, 1), (1, 0)])


def rows_of(column, copies):
    wide = jnp.broadcast_to(column, (256, 128))
    return [jnp.transpose(wide[h * 128 : (h + 1) * 128])[:1] for h in range(2)]


def fetch(lexicon, at, count, target, sems):
    copies = []
    for i in range(count):
        group = []
        for half in range(2):
            row = pl.multiple_of(number(*BLOCKS[at + i], half) * 256, 256)
            copy = pltpu.make_async_copy(
                lexicon.at[pl.ds(row, 256), :],
                target.at[pl.ds(i * 512 + half * 256, 256), :],
                sems.at[2 * i + half],
            )
            copy.start()
            group.append(copy)
        copies.append(group)
    return copies


def head_body(plan, *refs):
    sides, at, ready, following, first, last = plan
    refs = list(refs)
    take = lambda n: [refs.pop(0) for _ in range(n)]
    total = sum(sides)
    sources = take(len(sides))
    gain, lex_own, lex_peer = take(3)
    if not first:
        z_in, sq_in = take(2)
    if ready:
        (lexs,) = take(1)
    if last or following:
        sharp_ref, chosen_ref = take(2)
    if last:
        z_out, pick_out, lse_out, tok_out = take(4)
    else:
        z_out, pick_out, sq_out = take(3)
    if following:
        lex_next, sharp_out, chosen_out = take(3)
    if first:
        for source, copy_out in zip(sources, take(len(sources))):
            copy_out[...] = source[...]
    copies = None
    if not ready:
        lexs, sems = take(2)
        copies = fetch(lex_own, at, total, lexs, sems)
    if following:
        next_copies = fetch(lex_own, at + total, following, lex_next, *take(1))
    xs, held = take(2)
    x, c, t, y = place()
    mine = x * 4 + y
    squares = None if first else sq_in[...]
    own_piece, own_part = mine // 2, pl.multiple_of((mine % 2) * 16, 16)
    places = [(source, side) for source, some in zip(sources, sides) for side in range(some)]
    for start in range(0, total, 2):
        pair = range(start, min(start + 2, total))
        for i in pair:
            source, side = places[i]
            pick_out[i] = source[side, own_piece, :, pl.ds(own_part, 16), :]
            for j in range(4):
                wide = source[side, :, j].astype(F32).reshape(256, 128)
                squares = wide * wide if squares is None else squares + wide * wide
                row = gain[pl.ds(number(*BLOCKS[at + i], j // 2) * 2 + j % 2, 1), :]
                xs[:, i * 512 + j * 128 : i * 512 + (j + 1) * 128] = (wide * row).astype(BF16)
        if copies is not None:
            for i in pair:
                for copy in copies[i]:
                    copy.wait()
        span = slice(start * 512, (pair[-1] + 1) * 512)
        for side in range(2):
            cols = slice(side * 512, (side + 1) * 512)
            if side == 0:
                part = jnp.dot(xs[:, span], lexs[span, :], preferred_element_type=F32)
            else:
                part = 0.0
                for i in pair:
                    for half in range(2):
                        row = pl.multiple_of(number(*BLOCKS[at + i], half) * 256, 256)
                        x_cols = slice(i * 512 + half * 256, i * 512 + (half + 1) * 256)
                        part += jnp.dot(
                            xs[:, x_cols], lex_peer[pl.ds(row, 256), :], preferred_element_type=F32
                        )
            if start:
                z_out[:, cols] += part
            elif first:
                z_out[:, cols] = part
            else:
                z_out[:, cols] = z_in[:, cols] + part
    if not last:
        sq_out[...] = squares
    if following:
        sharp_out[...] = column_of(sharp_ref[...], held)
        chosen_out[...] = column_of(chosen_ref[...].astype(F32), held)
        for group in next_copies:
            for copy in group:
                copy.wait()
    if last:
        sharp = sharp_ref[...]
        chosen = chosen_ref[...].astype(jnp.int32)
        scale = lax.rsqrt(jnp.sum(squares, axis=1, keepdims=True) / 8192.0 + 1e-05) * sharp
        z = z_out[...] * scale
        z_out[...] = z
        top = jnp.max(z, axis=1, keepdims=True)
        lse = top + jnp.log(jnp.sum(jnp.exp(z - top), axis=1, keepdims=True))
        token = jnp.zeros((256, 1), F32)
        for side in range(2):
            base = (((x * 2 + (c if side == 0 else 1 - c)) * 8 + t) * 4 + y) * 512
            here = lax.broadcasted_iota(jnp.int32, (256, 512), 1) == chosen - base
            part = jnp.where(here, z[:, side * 512 : (side + 1) * 512], 0.0)
            token += jnp.sum(part, axis=1, keepdims=True)
        odd = lax.broadcasted_iota(jnp.int32, (256, 128), 0) % 2
        low, high = rows_of(lse, 256)
        lse_out[...] = jnp.where(odd == 0, low, high)
        low, high = rows_of(token, 256)
        tok_out[0:1, :] = low
        tok_out[1:2, :] = high


def head_call(sources, at, following, gain, lex_own, lex_peer, state, lexs, closing):
    sides = [source.shape[0] for source in sources]
    total = sum(sides)
    first, ready, last = state is None, lexs is not None, closing is not None and not following
    vmem, anywhere = pl.BlockSpec(), pl.BlockSpec(memory_space=pl.ANY)
    in_specs = [vmem] * (len(sources) + 1) + [anywhere, vmem]
    operands = [*sources, gain, in_hbm(lex_own), in_vmem(lex_peer)]
    for extra in (state, lexs, closing):
        if extra is not None:
            operands += list(extra)
            in_specs += [vmem] * len(extra)
    out_shape = [
        jax.ShapeDtypeStruct((256, 1024), F32),
        jax.ShapeDtypeStruct((total, 4, 16, 128), BF16),
    ]
    scratch = []
    if last:
        out_shape += [
            jax.ShapeDtypeStruct((256, 128), F32),
            jax.ShapeDtypeStruct((2, 128), F32),
        ]
    else:
        out_shape += [jax.ShapeDtypeStruct((256, 128), F32)]
    if following:
        out_shape += [pltpu.VMEM((512 * following, 512), BF16)]
        out_shape += [pltpu.VMEM((256, 1), F32)] * 2
    if first:
        out_shape += [jax.ShapeDtypeStruct(source.shape, source.dtype) for source in sources]
    if not ready:
        scratch += [pltpu.VMEM((512 * total, 512), BF16), pltpu.SemaphoreType.DMA((2 * total,))]
    if following:
        scratch += [pltpu.SemaphoreType.DMA((2 * following,))]
    scratch += [pltpu.VMEM((256, 512 * total), BF16), pltpu.VMEM((128, 128), F32)]
    return pl.pallas_call(
        functools.partial(head_body, (sides, at, ready, following, first, last)),
        in_specs=in_specs,
        out_shape=out_shape,
        scratch_shapes=scratch,
        compiler_params=pltpu.CompilerParams(vmem_limit_bytes=LIMIT),
        cost_estimate=pl.CostEstimate(
            flops=2 * 256 * 512 * 1024 * total,
            bytes_accessed=total * (2**20 + 2**18) + 2**21,
            transcendentals=0,
        ),
    )(*operands)


def pile_body(first_ref, second_ref, out_ref):
    out_ref[0] = first_ref[...]
    out_ref[1] = second_ref[...]


def pile(first, second):
    return pl.pallas_call(
        pile_body,
        out_shape=jax.ShapeDtypeStruct((2, 8, 4, 32, 128), BF16),
        compiler_params=pltpu.CompilerParams(vmem_limit_bytes=LIMIT),
        cost_estimate=pl.CostEstimate(flops=0, bytes_accessed=2**20, transcendentals=0),
    )(first, second)


def mass_body(z_ref, lse_ref, tok_ref, level_ref, *refs):
    picks, (out_ref, norm_out, hidden_out, heap, held) = refs[:-5], refs[-5:]
    at = 0
    for pick in picks:
        heap[at : at + pick.shape[0]] = pick[...]
        at += pick.shape[0]
    x, c, t, y = place()
    spots = [(far % 4, side % 4) for far, side in BLOCKS]
    for yb in range(4):
        dx, dy = (t // 2 - x + 4) % 4, (yb - y + 4) % 4
        far, side = jnp.where(c == 0, dx, dy), jnp.where(c == 0, dy, dx)
        spot = jnp.int32(0)
        for i, (f, s) in enumerate(spots):
            spot = jnp.where((far == f) & (side == s), i, spot)
        piece = heap[spot]
        for j in range(2):
            cols = slice(yb * 256 + j * 128, yb * 256 + (j + 1) * 128)
            hidden_out[:, cols] = jnp.where(t % 2 == c, piece[j], piece[2 + j])
    level = column_of(level_ref[...], held)
    parts = lse_ref[...]
    odd = lax.broadcasted_iota(jnp.int32, parts.shape, 0) % 2
    columns = []
    for h in range(2):
        top = jnp.max(jnp.where(odd == h, parts, -jnp.inf), axis=0, keepdims=True)
        total = jnp.sum(jnp.where(odd == h, jnp.exp(parts - top), 0.0), axis=0, keepdims=True)
        norm = top + jnp.log(total)
        norm_out[h : h + 1, :] = norm
        columns.append(jnp.transpose(jnp.broadcast_to(norm, (128, 128)))[:, :1])
    norms = jnp.concatenate(columns, axis=0)
    z = z_ref[...]
    slope = cut_slope / LN2
    offset = slope * norms - cut_slope * level
    kept = jnp.sum(jnp.exp(z - norms) / (1.0 + jnp.exp(offset - slope * z)), axis=1, keepdims=True)
    low, high = rows_of(kept, 512)
    which = lax.broadcasted_iota(jnp.int32, (512, 128), 0) % 4
    out_ref[...] = jnp.where(
        which == 0,
        low,
        jnp.where(which == 1, high, jnp.where(which == 2, tok_ref[0:1, :], tok_ref[1:2, :])),
    )


def mass_call(z, lse, tok, level, picks):
    return pl.pallas_call(
        mass_body,
        out_shape=[
            jax.ShapeDtypeStruct((512, 128), F32),
            jax.ShapeDtypeStruct((2, 128), F32),
            jax.ShapeDtypeStruct((16, 1024), BF16),
        ],
        scratch_shapes=[pltpu.VMEM((16, 4, 16, 128), BF16), pltpu.VMEM((128, 128), F32)],
        compiler_params=pltpu.CompilerParams(vmem_limit_bytes=LIMIT),
    )(z, lse, tok, level, *picks)


def swap_halves(rows):
    return jnp.concatenate([rows[:, 64:], rows[:, :64]], axis=1)


def surprise_body(got_ref, norm_ref, level_ref, out_ref):
    sums = jnp.sum(got_ref[...].reshape(64, 8, 128), axis=0)
    sums = sums[:4] + sums[4:]
    kept, token = sums[:2], sums[2:]
    table = level_ref[...]
    turned = swap_halves(table)
    even = lax.axis_index("core") == 0
    first, second = jnp.where(even, table, turned), jnp.where(even, turned, table)
    low = lax.broadcasted_iota(jnp.int32, (1, 128), 1) < 64
    level = jnp.concatenate(
        [jnp.where(low, first[2 * h : 2 * h + 1], second[2 * h + 1 : 2 * h + 2]) for h in range(2)]
    )
    token_logp = token - norm_ref[...]
    gate = cut_slope * (level + token_logp / LN2)
    log_gate = jnp.minimum(gate, 0.0) - jnp.log1p(jnp.exp(-jnp.abs(gate)))
    out_ref[...] = -(token_logp + log_gate - jnp.log(kept)) / LN2


def surprise_call(got, norm, level):
    return pl.pallas_call(
        surprise_body,
        out_shape=jax.ShapeDtypeStruct((2, 128), F32),
        compiler_params=pltpu.CompilerParams(vmem_limit_bytes=LIMIT),
    )(got, norm, level)


def merge_body(own_ref, peer_ref, level_ref, surprise_out, next_out):
    even = lax.axis_index("core") == 0
    own, peer = own_ref[...], peer_ref[...]
    evens, odds = jnp.where(even, own, peer), jnp.where(even, peer, own)
    low = lax.broadcasted_iota(jnp.int32, (1, 128), 1) < 64
    first = jnp.where(low, evens, swap_halves(odds))
    second = jnp.where(low, swap_halves(evens), odds)
    surprise = jnp.concatenate([first[:1], second[:1], first[1:], second[1:]])
    surprise_out[...] = surprise
    next_out[...] = level_ref[...] - 0.1 * (surprise - 5.0)


def merge_call(own, peer, level):
    return pl.pallas_call(
        merge_body,
        out_shape=[jax.ShapeDtypeStruct((4, 128), F32)] * 2,
        compiler_params=pltpu.CompilerParams(vmem_limit_bytes=LIMIT),
    )(own, peer, level)


def shards(
    probe_vectors,
    stored_lookup_vectors,
    stored_content_vectors,
    fresh_lookup_vector,
    fresh_content_vector,
    history_counts,
    mixing_matrix,
    skip_stream,
    closing_multiplier,
    lexicon_matrix,
    sharpening_factor,
    desired_perplexity,
    chosen_symbols,
):
    mix_peer = swap_core(mixing_matrix)

    sent, mix_own = attend(
        probe_vectors,
        stored_lookup_vectors,
        stored_content_vectors,
        fresh_lookup_vector,
        fresh_content_vector,
        history_counts,
        skip_stream,
        mixing_matrix,
    )
    lexicon_matrix, mix_peer, sent = lax.optimization_barrier((lexicon_matrix, mix_peer, sent))
    lex_peer = swap_core(lexicon_matrix)
    got = lax.all_to_all(sent, ("x", "rep"), 0, 0, tiled=True).reshape(256, 1280)
    gain_rows = closing_multiplier.reshape(8, 128)
    sent = project(got, mix_own, mix_peer, gain_rows)
    got = lax.all_to_all(sent, "tensor", 0, 0, tiled=True)
    sent, gain = total_call(got)

    own = lax.all_to_all(sent, "tensor", 0, 0, tiled=True).reshape(8, 4, 32, 128)
    side = lambda v, s: lax.ppermute(v, PLANE, turn_other(s))
    far = lambda v, s: lax.ppermute(v, PLANE, turn(s))
    ahead, behind, across = side(own, 1), side(own, -1), side(own, 2)
    low = pile(own, behind)
    ahead, across, low = lax.optimization_barrier((ahead, across, low))
    high = pile(ahead, across)
    left_low, right_high = far(low, 1), far(high, -1)
    past_low, past_high = far(left_low, 1), far(right_high, -1)

    fixed = (gain, lexicon_matrix, lex_peer)
    z, pick_0, sq, low, high = head_call([low, high], 0, 0, *fixed, None, None, None)
    left_high, right_low = far(high, 1), far(low, -1)
    z, pick_1, sq = head_call([left_low, right_high], 4, 0, *fixed, (z, sq), None, None)
    closing = (sharpening_factor.reshape(4, 128), chosen_symbols.reshape(4, 128))
    z, pick_2, sq, lexs, *closing = head_call(
        [left_high, right_low], 8, 4, *fixed, (z, sq), None, closing
    )
    z, pick_3, lse, tok = head_call(
        [past_low, past_high], 12, 0, *fixed, (z, sq), (lexs,), closing
    )
    picked = [pick_0, pick_1, pick_2, pick_3]
    every_lse = lax.all_to_all(lse.reshape(128, 2, 128), SAME_CORE, 0, 0, tiled=True)
    levels = desired_perplexity.reshape(4, 128)
    sent, norm, hidden = mass_call(z, every_lse.reshape(256, 128), tok, levels, picked)
    got = lax.all_to_all(sent.reshape(128, 4, 128), SAME_CORE, 0, 0, tiled=True)
    mine = surprise_call(got.reshape(512, 128), norm, levels)
    surprise, next_targets = merge_call(mine, swap_core(mine), levels)
    surprise, next_targets = surprise.reshape(512), next_targets.reshape(512)
    return (hidden, next_targets, surprise)


def solution(mesh):
    fine = Mesh(mesh.devices.reshape(4, 2, 8, 4), ("x", "core", "tensor", "rep"))
    rows = ("x", "core", "rep")
    placed = (
        P(rows, "tensor", None),
        P(rows, "tensor", None, None),
        P(rows, "tensor", None, None),
        P(rows, "tensor", None),
        P(rows, "tensor", None),
        P(rows),
        P("tensor", rows),
        P(rows, "tensor"),
        P("tensor"),
        P(None, ("x", "core", "tensor", "rep")),
        P(),
        P(),
        P(),
    )
    return jax.shard_map(
        shards,
        mesh=fine,
        in_specs=placed,
        out_specs=(P(rows, "tensor"), P(), P()),
        check_vma=False,
    )
```
